32 devices in a mesh: ctx: 2 (over x), exp: 16 (over z, y, core).
Axes of the slice: x: 2, y: 2, z: 4, core: 2. Of those that a mesh axis runs over, the one named last changes fastest.
Arguments:
- q_input: bfloat16 [1024, 8192], P('ctx', 'exp'), may hold values from -8 to 8
- k_input: bfloat16 [1024, 8192], P('ctx', 'exp'), may hold values from -8 to 8
- v_input: bfloat16 [1024, 8192], P('ctx', 'exp'), may hold values from -6 to 6
- segment_ids: int32 [1024], P('ctx'), may hold values from 0 to 5, never falling along the last dimension, each value on 1 to 512 neighbouring positions
- tokens: bfloat16 [1024, 5120], P('exp'), may hold values from -6 to 6
- expert_ids: int32 [1024, 6], P('exp'), may hold values from 0 to 15, all different within a row; in each aligned block of 64 rows (0 to 63, 64 to 127, ...) at most 32 rows name the same one
- route_weight: float32 [1024, 6], P('exp'), may hold values from 0.2 to 1
- w_in: bfloat16 [16, 2, 5120, 1536], P('exp', None, None, 'ctx'), may hold values from -0.078125 to 0.078125
- w_down: bfloat16 [16, 1536, 5120], P('exp', 'ctx'), may hold values from -0.15625 to 0.15625
Outputs:
- attn_out: bfloat16 [1024, 8192], P('ctx', 'exp')
- moe_out: bfloat16 [1024, 5120], P('exp', 'ctx')
The draws below stay inside these ranges and needn't reach their ends.
Inputs may be any that keep to these rules, and one draw needn't show every extreme that they name: `segment_ids`: never falling along the sequence; each document has 1 to 512 tokens, one exactly 512. `expert_ids`: each row names 6 different experts; in each aligned block of 64 rows no expert is named by more than 32 rows, a bound that some block reaches.
All inputs are finite; a program needn't handle non-finite values.
Results may differ from the reference program's by a relative error of at most 0.0066.
Values may be sent and summed in bfloat16 or wider, within the bound.
No kernel may reach another device: no remote copies, remote signals or barrier semaphores. Data moves between devices by JAX's collectives and lax.ppermute only.
A program may use at most 192 MiB of HBM per device.

```python
import math
import jax
import jax.numpy as jnp
import numpy as np
from jax import lax

D = 5120
FF = 1536
HD = 128
TOP = 6
HEADS = 64
EXPERTS = 16
TOKENS = 1024
ROWS = 64
CAP = 32
N_CTX = 2
N_EXP = 16


def draw_q_input(key, part):
    key = jax.random.fold_in(key, 11)
    base = jnp.clip(jax.random.normal(key, (TOKENS, HEADS * HD), jnp.float32), -6.0, 6.0)
    return base.astype(jnp.bfloat16)


def draw_k_input(key, part):
    key = jax.random.fold_in(key, 23)
    base = jnp.clip(jax.random.normal(key, (TOKENS, HEADS * HD), jnp.float32), -6.0, 6.0)
    return base.astype(jnp.bfloat16)


def steps_of(rng, extent, pieces, low, largest):
    def one(dim, blocks):
        draws = jax.random.uniform(jax.random.fold_in(jax.random.fold_in(rng, 6), dim), (blocks,), jnp.float32, low / len(pieces), largest / len(pieces))
        return jnp.repeat(jnp.exp(draws), extent[dim] // blocks).reshape((-1,) + (1,) * (len(extent) - dim - 1))

    level = one(*pieces[0])
    for cut in pieces[1:]:
        level = level * one(*cut)
    return level


def length_profile(count, total, bound, lean):
    weights = [(1 << 20) // math.isqrt(standing ** lean) + 1 for standing in range(2, count + 1)]
    surplus, counts = total - bound - (count - 1), [1] * (count - 1)
    while surplus > 0:
        free = [i for i in range(count - 1) if counts[i] < bound]
        mass, budget = sum([weights[i] for i in free]), surplus
        for i in free:
            extra = min(bound - counts[i], max(1, budget * weights[i] // mass), surplus)
            counts[i] = counts[i] + extra
            surplus = surplus - extra
    return np.array([bound] + counts)


def ragged(own_key, amount, total, reach, lean):
    if amount == 2:
        one = jax.random.randint(own_key, (), max(1, total - reach), min(reach, total - 1) + 1)
        return jnp.stack([one, total - one])
    sizes = jnp.asarray(length_profile(amount, total, reach, lean), jnp.int32)
    twos = (amount - 1) // 2
    giver, receiver = sizes[1:1 + 2 * twos:2], sizes[2:2 + 2 * twos:2]
    slack = jnp.minimum(giver - 1, reach - receiver)
    shifted = jax.random.randint(jax.random.fold_in(own_key, 1), (twos,), 0, 1 << 20) % (slack + 1)
    sizes = sizes.at[1:1 + 2 * twos:2].set(giver - shifted).at[2:2 + 2 * twos:2].set(receiver + shifted)
    return sizes[jax.random.permutation(jax.random.fold_in(own_key, 2), amount)]


def routed_block(key, own, number, rows, count, top, bound, skew):
    order = jax.random.permutation(key, count)
    packed, common = load_shares(count, rows * top, bound, skew, True), load_shares(count, rows * top, bound, skew, False)
    places = jnp.arange(count)

    def named(lengths, offset_by):
        used = int((lengths > 0).sum())
        fixed = max(1, used // 4)
        moved = fixed + (places - fixed + offset_by * (used - fixed)) % max(1, count - fixed)
        return jnp.zeros((count,), jnp.int32).at[order[jnp.where(places < fixed, places, moved)]].set(jnp.asarray(lengths, jnp.int32))

    lengths = jnp.where(number % 4 == 0, named(packed, number // 4), named(common, number - number // 4 - 1))
    mixed = jax.random.permutation(jax.random.fold_in(own, 3), count)
    donor, receiver = mixed[0:count // 2 * 2:2], mixed[1:count // 2 * 2:2]
    margin = jnp.minimum(lengths[donor] - 1, bound - lengths[receiver]) // 2
    margin = jnp.where((donor == order[0]) | (receiver == order[0]) | (lengths[receiver] == 0), 0, jnp.maximum(margin, 0))
    moved = jax.random.randint(jax.random.fold_in(own, 4), (count // 2,), 0, 1 << 20) % (margin + 1)
    lengths = lengths.at[donor].add(-moved).at[receiver].add(moved)
    members = jnp.searchsorted(jnp.cumsum(lengths), jnp.arange(rows * top), side="right").astype(jnp.int32)
    grid = members.reshape(top, rows).T
    grid = grid[jax.random.permutation(jax.random.fold_in(own, 1), rows)]
    offset_by = jax.random.randint(jax.random.fold_in(own, 2), (rows, 1), 0, top)
    return jnp.take_along_axis(grid, (jnp.arange(top)[None, :] + offset_by) % top, axis=1)


def load_shares(count, total, bound, skew, full):
    portions = [(1 << 20) // math.isqrt(grade ** skew) + 1 for grade in range(1, count + 1)]
    largest = bound if full else min(bound, max(-(-total // count), total * portions[0] // sum(portions)))
    least = 1 if total - largest >= count - 1 else 0
    given, spare = [largest] + [least] * (count - 1), total - largest - least * (count - 1)
    while spare > 0:
        movable = [i for i in range(1, count) if given[i] < largest] or [i for i in range(1, count) if given[i] < bound]
        pool, left = sum([portions[i] for i in movable]), spare
        for i in movable:
            addition = min(bound - given[i], max(1, left * portions[i] // pool), spare)
            given[i] = given[i] + addition
            spare = spare - addition
    return np.array(given)


def centred(key, extent, scale, bound, split=(), held_as=jnp.bfloat16):
    entries = jax.random.normal(key, extent, jnp.float32) * scale
    if len(split) > 0:
        entries = steps_of(key, extent, split, -0.22, 0.18) * entries
    return jnp.clip(entries, min=-bound, max=bound).astype(held_as)


def setup_inputs(seed: int = 0) -> dict:
    key_list = jax.random.split(jax.random.key(seed), 10)
    q_input = draw_q_input(jax.random.fold_in(key_list[9], 71), 0)
    k_input = draw_k_input(jax.random.fold_in(key_list[9], 71), 0)
    v_input = centred(key_list[2], (TOKENS, HEADS * HD), 1.0, 6.0, ((0, 2), (1, 16)))
    segment_ids = jnp.searchsorted(jnp.cumsum(ragged(key_list[3], 6, TOKENS, TOKENS // 2, 2)), jnp.arange(TOKENS), side="right").astype(jnp.int32)
    tokens = centred(key_list[4], (TOKENS, D), 1.0, 6.0, ((0, 16),))
    expert_ids_keys = jax.random.split(jax.random.fold_in(key_list[5], 1), TOKENS // ROWS)
    expert_ids_turns = jax.random.permutation(jax.random.fold_in(key_list[5], 3), TOKENS // ROWS)
    expert_ids = jax.vmap(lambda own, number: routed_block(jax.random.fold_in(key_list[5], 2), own, number, ROWS, EXPERTS, TOP, CAP, 2))(expert_ids_keys, expert_ids_turns).reshape((TOKENS, TOP))
    route_weight = jnp.clip(0.2 + 0.8 * jax.random.uniform(key_list[6], (TOKENS, TOP), jnp.float32) ** steps_of(key_list[6], (TOKENS, TOP), ((0, 16),), -0.2, 0.2), 0.2, 1.0)
    w_in = centred(key_list[7], (EXPERTS, 2, D, FF), D ** -0.5, 0.078125, ((0, 16), (3, 2)))
    w_down = centred(key_list[8], (EXPERTS, FF, D), FF ** -0.5, 0.15625, ((0, 16), (1, 2)))
    return dict(q_input=q_input, k_input=k_input, v_input=v_input, segment_ids=segment_ids, tokens=tokens, expert_ids=expert_ids, route_weight=route_weight, w_in=w_in, w_down=w_down)


def attention(q_input, k_input, v_input, segment_ids):
    scale = HD ** -0.5
    place = jnp.arange(TOKENS, dtype=jnp.int32)
    visible = (place[None, :] <= place[:, None]) & (segment_ids[None, :] == segment_ids[:, None])

    def one_head(head):
        start = (head * HD).astype(jnp.int32)
        query = lax.dynamic_slice_in_dim(q_input, start, HD, 1)
        keys = lax.dynamic_slice_in_dim(k_input, start, HD, 1)
        values = lax.dynamic_slice_in_dim(v_input, start, HD, 1)
        scores = jnp.dot(query, keys.T, preferred_element_type=jnp.float32) * scale
        scores = jnp.where(visible, scores, -jnp.inf)
        top = jnp.max(scores, axis=1, keepdims=True)
        probs = jnp.where(visible, jnp.exp(scores - top), 0.0)
        total = jnp.sum(probs, axis=1, keepdims=True)
        mixed = jnp.dot(probs.astype(jnp.bfloat16), values, preferred_element_type=jnp.float32) / total
        return mixed.astype(jnp.bfloat16)

    stacked = lax.map(one_head, jnp.arange(HEADS, dtype=jnp.int32))
    return jnp.transpose(stacked, (1, 0, 2)).reshape(TOKENS, HEADS * HD)


def experts_part(tokens, expert_ids, route_weight, w_in, w_down):
    flat = expert_ids.reshape(N_EXP, ROWS * TOP)
    onehot = (flat[:, :, None] == jnp.arange(EXPERTS, dtype=jnp.int32)[None, None, :]).astype(jnp.int32)
    rank = jnp.sum((jnp.cumsum(onehot, axis=1) - onehot) * onehot, axis=2)
    source = jnp.arange(N_EXP, dtype=jnp.int32)[:, None]
    dest = (flat * (N_EXP * CAP) + source * CAP + rank).reshape(TOKENS * TOP)
    filled = jnp.zeros((EXPERTS * N_EXP * CAP, D), jnp.bfloat16)
    filled = filled.at[dest].set(jnp.repeat(tokens, TOP, axis=0))
    filled = filled.reshape(EXPERTS, N_EXP * CAP, D)
    group = FF // N_CTX

    def one_expert(items):
        block, weights_in, weights_down = items
        gate = jnp.dot(block, weights_in[0], preferred_element_type=jnp.float32)
        up = jnp.dot(block, weights_in[1], preferred_element_type=jnp.float32)
        hidden = (jax.nn.silu(gate) * up).astype(jnp.bfloat16)
        parts = hidden.reshape(N_EXP * CAP, N_CTX, group).astype(jnp.float32)
        downs = weights_down.reshape(N_CTX, group, D).astype(jnp.float32)
        partial_value = jnp.einsum('scf,cfd->csd', parts, downs).astype(jnp.bfloat16)
        partial_value = lax.optimization_barrier(partial_value).astype(jnp.float32)
        return jnp.sum(partial_value, axis=0).astype(jnp.bfloat16)

    outputs = lax.map(one_expert, (filled, w_in, w_down)).reshape(EXPERTS * N_EXP * CAP, D)
    picked = outputs[dest].reshape(TOKENS, TOP, D).astype(jnp.float32)
    return jnp.sum(picked * route_weight[:, :, None], axis=1).astype(jnp.bfloat16)


def reference(q_input, k_input, v_input, segment_ids, tokens, expert_ids, route_weight, w_in, w_down):
    attn_out = attention(q_input, k_input, v_input, segment_ids)
    moe_out = experts_part(tokens, expert_ids, route_weight, w_in, w_down)
    return (attn_out, moe_out)
```

```python
import jax
import jax.numpy as jnp
from jax import lax
from jax.sharding import PartitionSpec as P

HD = 128
TOP = 6
BF16 = jnp.bfloat16
F32 = jnp.float32


def attend(q_input, k_input, v_input, segment_ids, n_ctx):
    scale = HD ** (-0.5)
    rows = q_input.shape[0]
    heads = q_input.shape[1] // HD
    place = lax.axis_index("ctx") * rows + jnp.arange(rows, dtype=jnp.int32)
    if n_ctx == 2:
        ahead = [(0, 1)]
        keys = jnp.concatenate([lax.ppermute(k_input, "ctx", ahead), k_input], axis=0)
        values = jnp.concatenate([lax.ppermute(v_input, "ctx", ahead), v_input], axis=0)
        docs = jnp.concatenate([lax.ppermute(segment_ids, "ctx", ahead), segment_ids], axis=0)
        first = (lax.axis_index("ctx") - 1) * rows
    else:
        keys = lax.all_gather(k_input, "ctx", axis=0, tiled=True)
        values = lax.all_gather(v_input, "ctx", axis=0, tiled=True)
        docs = lax.all_gather(segment_ids, "ctx", axis=0, tiled=True)
        first = 0
    count = keys.shape[0]
    key_place = first + jnp.arange(count, dtype=jnp.int32)
    visible = (
        (key_place[None, :] <= place[:, None])
        & (key_place[None, :] >= 0)
        & (docs[None, :] == segment_ids[:, None])
    )
    queries = q_input.reshape(rows, heads, HD)
    scores = (
        jnp.einsum(
            "qhd,khd->qhk", queries, keys.reshape(count, heads, HD), preferred_element_type=F32
        )
        * scale
    )
    scores = jnp.where(visible[:, None, :], scores, -1e30)
    newest = jnp.max(scores, axis=2)
    probs = jnp.where(visible[:, None, :], jnp.exp(scores - newest[:, :, None]), 0.0)
    total = jnp.sum(probs, axis=2)
    summed = jnp.einsum(
        "qhk,khd->qhd",
        probs.astype(BF16),
        values.reshape(count, heads, HD),
        preferred_element_type=F32,
    )
    return (summed / total[:, :, None]).reshape(rows, heads * HD).astype(BF16)


def spread(onehot):
    blocks, cap, rows = onehot.shape
    same = jnp.eye(blocks, dtype=jnp.bool_)
    wide = onehot[:, :, None, :] & same[:, None, :, None]
    return wide.reshape(blocks * cap, blocks * rows).astype(BF16)


def solution(mesh):
    n_ctx = mesh.shape["ctx"]
    n_exp = mesh.shape["exp"]
    nz = n_exp // 4

    def pairs(move):
        out = []
        for i in range(n_exp):
            z, y, c = i // 4, (i // 2) % 2, i % 2
            z, y, c = move(z, y, c)
            out.append((i, (z % nz * 2 + y) * 2 + c))
        return out

    def z_shift(x, d):
        return lax.ppermute(x, "exp", pairs(lambda z, y, c: (z + d, y, c)))

    def y_swap(x):
        return lax.ppermute(x, "exp", pairs(lambda z, y, c: (z, 1 - y, c)))

    def core_swap(x):
        return lax.ppermute(x, "exp", pairs(lambda z, y, c: (z, y, 1 - c)))

    def x_swap(x):
        return lax.ppermute(x, "ctx", [(0, 1), (1, 0)])

    def on_device(
        q_input, k_input, v_input, segment_ids, tokens, expert_ids, route_weight, w_in, w_down
    ):
        me = lax.axis_index("exp")
        at_x = lax.axis_index("ctx")
        rows, width = tokens.shape
        cap = rows * 8 // n_exp
        half = width // 2
        near = n_exp // 2
        slots = near * cap

        if n_ctx == 2:
            plan = [("x", 1024), ("x", 1024), ("", 1024), ("x", 1024), ("", 1024)]
        else:
            plan = [("", width)]
        arrived = []
        start = 0
        for kind, size in plan:
            if kind == "x":
                block = lax.dynamic_slice_in_dim(tokens, start + at_x * (size // 2), size // 2, 1)
            else:
                block = tokens[:, start : start + size]
            line = jnp.concatenate([block] + [z_shift(block, d) for d in range(1, nz)], axis=0)
            both = jnp.concatenate([line, y_swap(line)], axis=0)
            if kind == "x":
                other = x_swap(both)
                both = jnp.concatenate(
                    [jnp.where(at_x == 0, both, other), jnp.where(at_x == 0, other, both)], axis=1
                )
            arrived.append((start, size, both))
            start += size

        meta = jnp.concatenate([expert_ids.astype(F32), route_weight], axis=1)
        meta = lax.all_gather(meta, "exp", axis=0, tiled=False)
        z, y, c = me // 4, (me // 2) % 2, me % 2
        order = jnp.stack(
            [
                ((z - d + nz) % nz * 2 + (y + yr) % 2) * 2 + (c + cr) % 2
                for cr in range(2)
                for yr in range(2)
                for d in range(nz)
            ]
        )
        meta = meta[order]
        ids, weights = meta[:, :, :TOP].astype(jnp.int32), meta[:, :, TOP:]

        def placing(ids, expert):
            named = ids == expert
            hit = jnp.any(named, axis=2)
            count = hit.astype(jnp.int32)
            rank = jnp.cumsum(count, axis=1) - count
            slot = jnp.arange(cap, dtype=jnp.int32)
            return named, hit[:, None, :] & (rank[:, None, :] == slot[None, :, None])

        named, mine = placing(ids, me)
        _, others = placing(ids[:near], me + 1 - 2 * c)
        weight = jnp.sum(jnp.where(named, weights, 0.0), axis=2)
        weight = jnp.sum(jnp.where(mine, weight[:, None, :], 0.0), axis=2).reshape(2 * slots, 1)
        place = jnp.concatenate([spread(mine[:near]), spread(others)], axis=0)

        gate = up = None
        for start, size, both in arrived:
            placed = jnp.dot(place, both, preferred_element_type=F32).astype(BF16)
            block = jnp.concatenate([placed[:slots], core_swap(placed[slots:])], axis=0)
            g = jnp.dot(block, w_in[0, 0, start : start + size], preferred_element_type=F32)
            u = jnp.dot(block, w_in[0, 1, start : start + size], preferred_element_type=F32)
            gate = g if gate is None else gate + g
            up = u if up is None else up + u
        hidden = (jax.nn.silu(gate) * up).astype(BF16)

        if n_ctx == 2:
            back = [("x", 512), ("x", 512), ("", 512), ("x", 512), ("", 512)]
        else:
            back = [("", half)]
        down = w_down[0]
        pieces = []
        start = 0
        for kind, size in back:
            if n_ctx == 2:
                cols = jnp.concatenate(
                    [down[:, start : start + size], down[:, half + start : half + start + size]],
                    axis=1,
                )
            else:
                cols = down
            part = jnp.dot(hidden, cols, preferred_element_type=F32)
            part = (part * weight).astype(BF16)
            part = jnp.concatenate([part[:slots], core_swap(part[slots:])], axis=0)
            summed = lax.dot_general(
                place, part, (((0,), (0,)), ((), ())), preferred_element_type=F32
            )

            def over_x(summed):
                first, second = summed[:, :size].astype(BF16), summed[:, size:].astype(BF16)
                other = x_swap(jnp.where(at_x == 0, second, first))
                own = jnp.where(at_x == 0, summed[:, :size], summed[:, size:])
                return own + other.astype(F32)

            if kind == "x":
                summed = over_x(summed)
            count = nz * rows
            summed = summed[:count] + y_swap(summed[count:].astype(BF16)).astype(F32)
            total = summed[:rows]
            for d in range(1, nz):
                block = summed[d * rows : (d + 1) * rows].astype(BF16)
                total = total + z_shift(block, -d).astype(F32)
            if kind != "x":
                if n_ctx == 2:
                    total = over_x(total)
                else:
                    total = lax.psum_scatter(
                        total.astype(BF16), "ctx", scatter_dimension=1, tiled=True
                    )
            pieces.append(total.astype(BF16))
            start += size
        moe_out = jnp.concatenate(pieces, axis=1)
        attn_out = attend(q_input, k_input, v_input, segment_ids, n_ctx)
        return attn_out, moe_out

    in_specs = (
        P("ctx", "exp"),
        P("ctx", "exp"),
        P("ctx", "exp"),
        P("ctx"),
        P("exp", None),
        P("exp", None),
        P("exp", None),
        P("exp", None, None, "ctx"),
        P("exp", "ctx", None),
    )
    out_specs = (P("ctx", "exp"), P("exp", "ctx"))
    return jax.shard_map(
        on_device, mesh=mesh, in_specs=in_specs, out_specs=out_specs, check_vma=False
    )
```

```python
import jax
import jax.numpy as jnp
from jax import lax
from jax.experimental import pallas as pl
from jax.experimental.pallas import tpu as pltpu
from jax.sharding import PartitionSpec as P

HD = 128
TOP = 6
BF16 = jnp.bfloat16
F32 = jnp.float32


def attend(q_input, k_input, v_input, segment_ids, n_ctx):
    scale = HD ** (-0.5)
    rows = q_input.shape[0]
    heads = q_input.shape[1] // HD
    place = lax.axis_index("ctx") * rows + jnp.arange(rows, dtype=jnp.int32)
    if n_ctx == 2:
        ahead = [(0, 1)]
        keys = jnp.concatenate([lax.ppermute(k_input, "ctx", ahead), k_input], axis=0)
        values = jnp.concatenate([lax.ppermute(v_input, "ctx", ahead), v_input], axis=0)
        docs = jnp.concatenate([lax.ppermute(segment_ids, "ctx", ahead), segment_ids], axis=0)
        first = (lax.axis_index("ctx") - 1) * rows
    else:
        keys = lax.all_gather(k_input, "ctx", axis=0, tiled=True)
        values = lax.all_gather(v_input, "ctx", axis=0, tiled=True)
        docs = lax.all_gather(segment_ids, "ctx", axis=0, tiled=True)
        first = 0
    count = keys.shape[0]
    key_place = first + jnp.arange(count, dtype=jnp.int32)
    visible = (
        (key_place[None, :] <= place[:, None])
        & (key_place[None, :] >= 0)
        & (docs[None, :] == segment_ids[:, None])
    )
    queries = q_input.reshape(rows, heads, HD)
    scores = (
        jnp.einsum(
            "qhd,khd->qhk", queries, keys.reshape(count, heads, HD), preferred_element_type=F32
        )
        * scale
    )
    scores = jnp.where(visible[:, None, :], scores, -1e30)
    newest = jnp.max(scores, axis=2)
    probs = jnp.where(visible[:, None, :], jnp.exp(scores - newest[:, :, None]), 0.0)
    total = jnp.sum(probs, axis=2)
    summed = jnp.einsum(
        "qhk,khd->qhd",
        probs.astype(BF16),
        values.reshape(count, heads, HD),
        preferred_element_type=F32,
    )
    return (summed / total[:, :, None]).reshape(rows, heads * HD).astype(BF16)

SHARED = 2048
OVER_X = 1536
Z_ORDER = [1, 3, 2]
GROUPS = [[0, 1, 3, 2]]
BACK = [2, 1, 3, 0]

VMEM = pl.BlockSpec(memory_space=pltpu.VMEM)
ROOM = 48 * 1024 * 1024
LANES = 128


def call(body, out_shape, flops, moved, **kw):
    return pl.pallas_call(
        body,
        out_shape=out_shape,
        compiler_params=pltpu.CompilerParams(vmem_limit_bytes=ROOM),
        cost_estimate=pl.CostEstimate(flops=flops, bytes_accessed=moved, transcendentals=0),
        **kw,
    )


def pick(blocks, me, cap, experts):
    count = len(blocks)
    rows, width = blocks[0].shape

    def body(me_ref, *refs):
        ins, (near, other, placing) = refs[:count], refs[count:]
        mine = me_ref[0]
        lane = lax.broadcasted_iota(jnp.int32, (rows, LANES), 1)
        earlier = lax.broadcasted_iota(jnp.int32, (rows, rows), 0) > lax.broadcasted_iota(
            jnp.int32, (rows, rows), 1
        )
        slot = lax.broadcasted_iota(jnp.int32, (rows, cap), 1).astype(F32)
        for i, ref in enumerate(ins):
            member = ref[:, width - LANES :]
            rank = jnp.dot(earlier.astype(BF16), member, preferred_element_type=F32)
            member = member.astype(F32)
            for j, out in enumerate((near, other)):
                at = lane == (mine if j == 0 else mine + 1 - 2 * (mine % 2))
                hit = jnp.sum(jnp.where(at, member, 0.0), axis=1, keepdims=True)
                place = jnp.sum(jnp.where(at, rank, 0.0), axis=1, keepdims=True)
                onehot = jnp.where((place == slot) & (hit > 0.5), 1.0, 0.0).astype(BF16)
                placing[i, :, j * cap : (j + 1) * cap] = onehot
                out[i * cap : (i + 1) * cap, :] = lax.dot_general(
                    onehot, ref[...], (((0,), (0,)), ((), ())), preferred_element_type=F32
                ).astype(BF16)

    slots = jax.ShapeDtypeStruct((count * cap, width), BF16)
    return call(
        body,
        (slots, slots, jax.ShapeDtypeStruct((count, rows, 2 * cap), BF16)),
        4 * count * cap * rows * width,
        2 * count * (rows + 2 * cap) * width,
        in_specs=[pl.BlockSpec(memory_space=pltpu.SMEM)] + [VMEM] * count,
        out_specs=(VMEM,) * 3,
    )(me.reshape(1), *blocks)


def pick_more(arrays, placing, cap):
    total, rows, _ = placing.shape
    width = arrays[0].shape[1]

    def body(placing, *refs):
        ins, (near, other) = refs[:-2], refs[-2:]
        i = 0
        for ref in ins:
            for b in range(ref.shape[0] // rows):
                for j, out in enumerate((near, other)):
                    out[i * cap : (i + 1) * cap, :] = lax.dot_general(
                        placing[i, :, j * cap : (j + 1) * cap],
                        ref[b * rows : (b + 1) * rows, :],
                        (((0,), (0,)), ((), ())),
                        preferred_element_type=F32,
                    ).astype(BF16)
                i += 1

    slots = jax.ShapeDtypeStruct((total * cap, width), BF16)
    return call(
        body,
        (slots, slots),
        4 * total * cap * rows * width,
        2 * total * (rows + 2 * cap) * width,
        in_specs=[VMEM] * (1 + len(arrays)),
        out_specs=(VMEM,) * 2,
    )(placing, *arrays)


def widen(near, near_x, far, far_x, w_in, me, at_x, shared, split, experts, tile=512):
    slots = near.shape[0]
    width = near.shape[1]
    units = w_in.shape[3]
    main, more = (shared + split) // tile, split // tile
    steps = main + more

    def place(k, s):
        first, own, other = shared // tile, s[1] * more, (1 - s[1]) * more
        return jnp.where(
            k < first, k, jnp.where(k < main, own + k, other + k - more)
        )

    def body(s, near, near_x, far, far_x, w, hidden, weight, gate, up):
        k = pl.program_id(0)

        @pl.when(k == 0)
        def _():
            gate[...] = jnp.zeros_like(gate)
            up[...] = jnp.zeros_like(up)
            lane = lax.broadcasted_iota(jnp.int32, (slots, LANES), 1)
            at = (lane % experts == s[0]) & (lane >= experts) & (lane < 4 * experts)
            for i, ref in enumerate((near, far)):
                meta = ref[:, width - LANES :].astype(F32)
                weight[i * slots : (i + 1) * slots, :] = jnp.sum(
                    jnp.where(at, meta, 0.0), axis=1, keepdims=True
                )

        def add(a, b, column):
            columns = pl.ds(pl.multiple_of(column, tile), tile)
            block = jnp.concatenate([a[:, columns], b[:, columns]], axis=0)
            gate[...] += jnp.dot(block, w[0, 0], preferred_element_type=F32)
            up[...] += jnp.dot(block, w[0, 1], preferred_element_type=F32)

        @pl.when(k < main)
        def _():
            add(near, far, k * tile)

        @pl.when(k >= main)
        def _():
            add(near_x, far_x, (k - main) * tile)

        @pl.when(k == steps - 1)
        def _():
            hidden[...] = (jax.nn.silu(gate[...]) * up[...]).astype(BF16)

    whole = lambda shape: pl.BlockSpec(shape, lambda k, s: (0,) * len(shape))
    return call(
        body,
        (
            jax.ShapeDtypeStruct((2 * slots, units), BF16),
            jax.ShapeDtypeStruct((2 * slots, 1), F32),
        ),
        8 * slots * units * steps * tile,
        4 * units * steps * tile,
        grid_spec=pltpu.PrefetchScalarGridSpec(
            num_scalar_prefetch=1,
            grid=(steps,),
            in_specs=[whole(a.shape) for a in (near, near_x, far, far_x)]
            + [pl.BlockSpec((1, 2, tile, units), lambda k, s: (0, 0, place(k, s), 0))],
            out_specs=(whole((2 * slots, units)), whole((2 * slots, 1))),
            scratch_shapes=[pltpu.VMEM((2 * slots, units), F32)] * 2,
        ),
    )(jnp.stack([me, at_x]), near, near_x, far, far_x, w_in)


def narrow(hidden, weight, w_down, at_x, columns, tile):
    slots, units = hidden.shape
    slots = slots // 2
    steps = len(columns[0])
    table = jnp.where(at_x == 0, jnp.array(columns[0], jnp.int32), jnp.array(columns[1], jnp.int32))

    def body(s, hidden, weight, w, near, far):
        out = jnp.dot(hidden[...], w[0], preferred_element_type=F32) * weight[...]
        near[...] = out[:slots].astype(BF16)
        far[...] = out[slots:].astype(BF16)

    out = jax.ShapeDtypeStruct((slots, steps * tile), BF16)
    return call(
        body,
        (out, out),
        4 * slots * units * steps * tile,
        2 * units * steps * tile + 4 * slots * steps * tile,
        grid_spec=pltpu.PrefetchScalarGridSpec(
            num_scalar_prefetch=1,
            grid=(steps,),
            in_specs=[
                pl.BlockSpec(hidden.shape, lambda n, s: (0, 0)),
                pl.BlockSpec(weight.shape, lambda n, s: (0, 0)),
                pl.BlockSpec((1, units, tile), lambda n, s: (0, 0, s[n])),
            ],
            out_specs=(pl.BlockSpec((slots, tile), lambda n, s: (0, n)),) * 2,
        ),
    )(table, hidden, weight, w_down)


def mix(placing, near, far, first, count, adds=(), dtype=BF16):
    _, rows, both = placing.shape
    cap = both // 2
    width = near.shape[1]

    def body(placing, near, far, *refs):
        slots = jnp.concatenate([near[...], far[...]], axis=0)
        total = jnp.dot(placing[0], slots, preferred_element_type=F32)
        narrow = [r for r in refs[:-1] if r.shape[1] < width]
        full = [r for r in refs[:-1] if r.shape[1] == width]
        out = refs[-1]
        for ref in full:
            total = total + ref[...].astype(F32)
        if narrow:
            edge = narrow[0].shape[1]
            left = total[:, :edge]
            for ref in narrow:
                left = left + ref[...].astype(F32)
            out[:, :edge] = left.astype(dtype)
            out[:, edge:] = total[:, edge:].astype(dtype)
        else:
            out[...] = total.astype(dtype)

    def at(base):
        return lambda g: (g + base, 0)

    return call(
        body,
        jax.ShapeDtypeStruct((count * rows, width), dtype),
        4 * count * rows * cap * width,
        2 * count * (rows + 2 * cap) * width,
        grid=(count,),
        in_specs=[
            pl.BlockSpec((1, rows, both), lambda g: (g + first, 0, 0)),
            pl.BlockSpec((cap, width), at(first)),
            pl.BlockSpec((cap, width), at(first)),
        ]
        + [pl.BlockSpec((rows, a.shape[1]), at(base)) for a, base in adds],
        out_specs=pl.BlockSpec((rows, width), at(0)),
    )(placing, near, far, *[a for a, _ in adds])


def spread(onehot):
    blocks, cap, rows = onehot.shape
    same = jnp.eye(blocks, dtype=jnp.bool_)
    wide = onehot[:, :, None, :] & same[:, None, :, None]
    return wide.reshape(blocks * cap, blocks * rows).astype(BF16)


def solution(mesh):
    n_ctx = mesh.shape["ctx"]
    n_exp = mesh.shape["exp"]
    nz = n_exp // 4

    def pairs(move):
        out = []
        for i in range(n_exp):
            z, y, c = i // 4, (i // 2) % 2, i % 2
            z, y, c = move(z, y, c)
            out.append((i, (z % nz * 2 + y) * 2 + c))
        return out

    def z_shift(x, d):
        return lax.ppermute(x, "exp", pairs(lambda z, y, c: (z + d, y, c)))

    def y_swap(x):
        return lax.ppermute(x, "exp", pairs(lambda z, y, c: (z, 1 - y, c)))

    def core_swap(x):
        return lax.ppermute(x, "exp", pairs(lambda z, y, c: (z, y, 1 - c)))

    def x_swap(x):
        return lax.ppermute(x, "ctx", [(0, 1), (1, 0)])

    def on_device(
        q_input, k_input, v_input, segment_ids, tokens, expert_ids, route_weight, w_in, w_down
    ):
        me = lax.axis_index("exp")
        at_x = lax.axis_index("ctx")
        rows, width = tokens.shape
        cap = rows * 8 // n_exp
        half = width // 2
        near = n_exp // 2
        slots = near * cap

        if n_ctx == 2:
            plan = [("x", 1024), ("x", 1024), ("", 1024), ("x", 1024), ("", 1024)]
        else:
            plan = [("", width)]
        arrived = []
        start = 0
        for kind, size in plan:
            if kind == "x":
                block = lax.dynamic_slice_in_dim(tokens, start + at_x * (size // 2), size // 2, 1)
            else:
                block = tokens[:, start : start + size]
            line = jnp.concatenate([block] + [z_shift(block, d) for d in range(1, nz)], axis=0)
            both = jnp.concatenate([line, y_swap(line)], axis=0)
            if kind == "x":
                other = x_swap(both)
                both = jnp.concatenate(
                    [jnp.where(at_x == 0, both, other), jnp.where(at_x == 0, other, both)], axis=1
                )
            arrived.append((start, size, both))
            start += size

        meta = jnp.concatenate([expert_ids.astype(F32), route_weight], axis=1)
        meta = lax.all_gather(meta, "exp", axis=0, tiled=False)
        z, y, c = me // 4, (me // 2) % 2, me % 2
        order = jnp.stack(
            [
                ((z - d + nz) % nz * 2 + (y + yr) % 2) * 2 + (c + cr) % 2
                for cr in range(2)
                for yr in range(2)
                for d in range(nz)
            ]
        )
        meta = meta[order]
        ids, weights = meta[:, :, :TOP].astype(jnp.int32), meta[:, :, TOP:]

        def placing(ids, expert):
            named = ids == expert
            hit = jnp.any(named, axis=2)
            count = hit.astype(jnp.int32)
            rank = jnp.cumsum(count, axis=1) - count
            slot = jnp.arange(cap, dtype=jnp.int32)
            return named, hit[:, None, :] & (rank[:, None, :] == slot[None, :, None])

        named, mine = placing(ids, me)
        _, others = placing(ids[:near], me + 1 - 2 * c)
        weight = jnp.sum(jnp.where(named, weights, 0.0), axis=2)
        weight = jnp.sum(jnp.where(mine, weight[:, None, :], 0.0), axis=2).reshape(2 * slots, 1)
        place = jnp.concatenate([spread(mine[:near]), spread(others)], axis=0)

        gate = up = None
        for start, size, both in arrived:
            placed = jnp.dot(place, both, preferred_element_type=F32).astype(BF16)
            block = jnp.concatenate([placed[:slots], core_swap(placed[slots:])], axis=0)
            g = jnp.dot(block, w_in[0, 0, start : start + size], preferred_element_type=F32)
            u = jnp.dot(block, w_in[0, 1, start : start + size], preferred_element_type=F32)
            gate = g if gate is None else gate + g
            up = u if up is None else up + u
        hidden = (jax.nn.silu(gate) * up).astype(BF16)

        if n_ctx == 2:
            back = [("x", 512), ("x", 512), ("", 512), ("x", 512), ("", 512)]
        else:
            back = [("", half)]
        down = w_down[0]
        pieces = []
        start = 0
        for kind, size in back:
            if n_ctx == 2:
                cols = jnp.concatenate(
                    [down[:, start : start + size], down[:, half + start : half + start + size]],
                    axis=1,
                )
            else:
                cols = down
            part = jnp.dot(hidden, cols, preferred_element_type=F32)
            part = (part * weight).astype(BF16)
            part = jnp.concatenate([part[:slots], core_swap(part[slots:])], axis=0)
            summed = lax.dot_general(
                place, part, (((0,), (0,)), ((), ())), preferred_element_type=F32
            )

            def over_x(summed):
                first, second = summed[:, :size].astype(BF16), summed[:, size:].astype(BF16)
                other = x_swap(jnp.where(at_x == 0, second, first))
                own = jnp.where(at_x == 0, summed[:, :size], summed[:, size:])
                return own + other.astype(F32)

            if kind == "x":
                summed = over_x(summed)
            count = nz * rows
            summed = summed[:count] + y_swap(summed[count:].astype(BF16)).astype(F32)
            total = summed[:rows]
            for d in range(1, nz):
                block = summed[d * rows : (d + 1) * rows].astype(BF16)
                total = total + z_shift(block, -d).astype(F32)
            if kind != "x":
                if n_ctx == 2:
                    total = over_x(total)
                else:
                    total = lax.psum_scatter(
                        total.astype(BF16), "ctx", scatter_dimension=1, tiled=True
                    )
            pieces.append(total.astype(BF16))
            start += size
        moe_out = jnp.concatenate(pieces, axis=1)
        attn_out = attend(q_input, k_input, v_input, segment_ids, n_ctx)
        return attn_out, moe_out

    def pair_device(
        q_input, k_input, v_input, segment_ids, tokens, expert_ids, route_weight, w_in, w_down
    ):
        me = lax.axis_index("exp")
        at_x = lax.axis_index("ctx")
        rows, width = tokens.shape
        cap = rows * 8 // n_exp
        half = width // 2

        named = expert_ids[:, :, None] == jnp.arange(n_exp, dtype=jnp.int32)
        member = jnp.any(named, axis=1).astype(F32)
        weight = jnp.sum(jnp.where(named, route_weight[:, :, None], 0.0), axis=1)
        high = lax.reduce_precision(weight, 8, 7)
        middle = lax.reduce_precision(weight - high, 8, 7)
        low = weight - high - middle
        meta = jnp.concatenate([member, high, middle, low], axis=1).astype(BF16)
        meta = jnp.pad(meta, ((0, 0), (0, LANES - meta.shape[1])))

        split = (width - SHARED) // 2
        mine = lax.dynamic_slice_in_dim(tokens, SHARED + at_x * split, split, 1)
        theirs = lax.dynamic_slice_in_dim(tokens, SHARED + (1 - at_x) * split, split, 1)
        block = jnp.concatenate([tokens[:, :SHARED], mine, meta], axis=1)
        line = {0: block}
        for d in Z_ORDER:
            line[d] = z_shift(block, d)
        across = {d: y_swap(line[d]) for d in [0] + Z_ORDER}
        cut = lambda a: a[:, SHARED : SHARED + split]
        more = {0: [theirs, x_swap(cut(across[0]))]}
        for d in Z_ORDER:
            more[d] = [x_swap(jnp.concatenate([cut(line[d]), cut(across[d])], axis=0))]

        tile = 512
        per = half // tile
        first = OVER_X // tile
        lists = []
        for x in range(2):
            own, other = x * per, (1 - x) * per
            late = [other + n for n in range(first)]
            main = [own + n for n in range(per)] + [other + n for n in range(first, per)]
            lists.append((late, main))

        done = {}
        for group in GROUPS:
            near, out, placing = pick(
                [b for d in group for b in (line[d], across[d])], me, cap, n_exp
            )
            near_x, out_x = pick_more([a for d in group for a in more[d]], placing, cap)
            far, far_x = core_swap(out), core_swap(out_x)
            hidden, scale = widen(
                near, near_x, far, far_x, w_in, me, at_x, SHARED, split, n_exp
            )
            near_l, out_l = narrow(hidden, scale, w_down, at_x, [l[0] for l in lists], tile)
            far_l = core_swap(out_l)
            near_m, out_m = narrow(hidden, scale, w_down, at_x, [l[1] for l in lists], tile)
            far_m = core_swap(out_m)
            for i, d in sorted(enumerate(group), key=lambda p: BACK.index(p[1])):
                b = 2 * i
                got_x = x_swap(mix(placing, near_l, far_l, b, 2))
                got_y = y_swap(mix(placing, near_m, far_m, b + 1, 1, [(got_x, 1)]))
                sums = mix(
                    placing,
                    near_m,
                    far_m,
                    b,
                    1,
                    [(got_x, 0), (got_y, 0)],
                    F32 if d == 0 else BF16,
                )
                done[d] = sums if d == 0 else z_shift(sums, -d)
        total = done[0]
        for d in Z_ORDER:
            total = total + done[d].astype(F32)
        got = x_swap(total[:, half:].astype(BF16))
        moe_out = jnp.concatenate(
            [total[:, :OVER_X], total[:, OVER_X:half] + got.astype(F32)], axis=1
        ).astype(BF16)
        attn_out = attend(q_input, k_input, v_input, segment_ids, n_ctx)
        return attn_out, moe_out

    in_specs = (
        P("ctx", "exp"),
        P("ctx", "exp"),
        P("ctx", "exp"),
        P("ctx"),
        P("exp", None),
        P("exp", None),
        P("exp", None),
        P("exp", None, None, "ctx"),
        P("exp", "ctx", None),
    )
    out_specs = (P("ctx", "exp"), P("exp", "ctx"))
    return jax.shard_map(
        pair_device if n_ctx == 2 else on_device,
        mesh=mesh,
        in_specs=in_specs,
        out_specs=out_specs,
        check_vma=False,
    )
```

```python
import jax
import jax.numpy as jnp
from jax import lax
from jax.experimental import pallas as pl
from jax.experimental.pallas import tpu as pltpu
from jax.sharding import PartitionSpec as P

HD = 128
TOP = 6
BF16 = jnp.bfloat16
F32 = jnp.float32


def attend(q_input, k_input, v_input, segment_ids, n_ctx):
    scale = HD ** (-0.5)
    rows = q_input.shape[0]
    heads = q_input.shape[1] // HD
    place = lax.axis_index("ctx") * rows + jnp.arange(rows, dtype=jnp.int32)
    if n_ctx == 2:
        ahead = [(0, 1)]
        keys = jnp.concatenate([lax.ppermute(k_input, "ctx", ahead), k_input], axis=0)
        values = jnp.concatenate([lax.ppermute(v_input, "ctx", ahead), v_input], axis=0)
        docs = jnp.concatenate([lax.ppermute(segment_ids, "ctx", ahead), segment_ids], axis=0)
        first = (lax.axis_index("ctx") - 1) * rows
    else:
        keys = lax.all_gather(k_input, "ctx", axis=0, tiled=True)
        values = lax.all_gather(v_input, "ctx", axis=0, tiled=True)
        docs = lax.all_gather(segment_ids, "ctx", axis=0, tiled=True)
        first = 0
    count = keys.shape[0]
    key_place = first + jnp.arange(count, dtype=jnp.int32)
    visible = (
        (key_place[None, :] <= place[:, None])
        & (key_place[None, :] >= 0)
        & (docs[None, :] == segment_ids[:, None])
    )
    queries = q_input.reshape(rows, heads, HD)
    scores = (
        jnp.einsum(
            "qhd,khd->qhk", queries, keys.reshape(count, heads, HD), preferred_element_type=F32
        )
        * scale
    )
    scores = jnp.where(visible[:, None, :], scores, -1e30)
    newest = jnp.max(scores, axis=2)
    probs = jnp.where(visible[:, None, :], jnp.exp(scores - newest[:, :, None]), 0.0)
    total = jnp.sum(probs, axis=2)
    summed = jnp.einsum(
        "qhk,khd->qhd",
        probs.astype(BF16),
        values.reshape(count, heads, HD),
        preferred_element_type=F32,
    )
    return (summed / total[:, :, None]).reshape(rows, heads * HD).astype(BF16)

SHARED = 1280
OVER_X = 1536
ORDER = [2, 1, 3, 0]

VMEM = pl.BlockSpec(memory_space=pltpu.VMEM)
SMEM = pl.BlockSpec(memory_space=pltpu.SMEM)
MIB = 1024 * 1024
LANES = 128


def call(body, out_shape, flops, moved, room, **kw):
    return pl.pallas_call(
        body,
        out_shape=out_shape,
        compiler_params=pltpu.CompilerParams(vmem_limit_bytes=room * MIB),
        cost_estimate=pl.CostEstimate(flops=flops, bytes_accessed=moved, transcendentals=0),
        **kw,
    )


def prepare(tokens, expert_ids, route_weight, at_x, experts):
    rows, width = tokens.shape
    split = (width - SHARED) // 2

    def body(x_ref, tokens, ids, weights, out, theirs):
        own = pl.ds(pl.multiple_of(SHARED + x_ref[0] * split, LANES), split)
        other = pl.ds(pl.multiple_of(SHARED + (1 - x_ref[0]) * split, LANES), split)
        out[:, :SHARED] = tokens[:, :SHARED]
        out[:, SHARED : SHARED + split] = tokens[:, own]
        theirs[...] = tokens[:, other]
        column = lax.broadcasted_iota(jnp.int32, (LANES, rows), 0)
        expert, term = column % experts, column // experts
        meta = jnp.zeros((LANES, rows), F32)
        for k in range(TOP):
            weight = jnp.broadcast_to(weights[k : k + 1, :], (LANES, rows))
            high = weight.astype(BF16).astype(F32)
            middle = (weight - high).astype(BF16).astype(F32)
            low = weight - high - middle
            value = jnp.where(term == 1, high, jnp.where(term == 2, middle, low))
            value = jnp.where(term == 0, 1.0, value)
            meta = jnp.where((ids[k : k + 1, :] == expert) & (term < 4), value, meta)
        eye = lax.broadcasted_iota(jnp.int32, (LANES, LANES), 0) == lax.broadcasted_iota(
            jnp.int32, (LANES, LANES), 1
        )
        meta = lax.dot_general(
            meta.astype(BF16),
            jnp.where(eye, 1.0, 0.0).astype(BF16),
            (((0,), (0,)), ((), ())),
            preferred_element_type=F32,
        )
        out[:, SHARED + split :] = meta.astype(BF16)

    return call(
        body,
        (
            jax.ShapeDtypeStruct((rows, SHARED + split + LANES), BF16),
            jax.ShapeDtypeStruct((rows, split), BF16),
        ),
        0,
        4 * rows * width,
        8,
        in_specs=[SMEM] + [VMEM] * 3,
        out_specs=(VMEM,) * 2,
    )(at_x.reshape(1), tokens, expert_ids.T, route_weight.T)


def pick(blocks, more, me, at_x, cap):
    count = len(blocks)
    rows, width = blocks[0].shape
    split = more[0].shape[1]
    edge = width - LANES
    features = edge + split
    step = 4
    total = count + len(more)

    def body(s_ref, *refs):
        sources, (near, meta, other, placing, wide, *held, done) = refs[:total], refs[total:]
        copies = [
            pltpu.make_async_copy(source, to, done.at[i])
            for i, (source, to) in enumerate(zip(sources, held))
        ]
        for copy in copies:
            copy.start()
        for copy in copies:
            copy.wait()
        ins, extra = held[:count], held[count:]
        mine, x = s_ref[0], s_ref[1]
        lane = lax.broadcasted_iota(jnp.int32, (rows, LANES), 1)
        earlier = lax.broadcasted_iota(jnp.int32, (rows, rows), 0) > lax.broadcasted_iota(
            jnp.int32, (rows, rows), 1
        )
        slot = lax.broadcasted_iota(jnp.int32, (rows, cap), 1).astype(F32)
        own = pl.ds(pl.multiple_of(SHARED + x * split, LANES), split)
        theirs = pl.ds(pl.multiple_of(SHARED + (1 - x) * split, LANES), split)
        pieces = [
            ref[b * rows : (b + 1) * rows, :] for ref in extra for b in range(ref.shape[0] // rows)
        ]
        for begin in range(0, count, step):
            wide[...] = jnp.zeros_like(wide)
            for i in range(begin, begin + step):
                member = ins[i][:, edge:]
                rank = jnp.dot(earlier.astype(BF16), member, preferred_element_type=F32)
                member = member.astype(F32)
                local = i - begin
                for j in range(2):
                    at = lane == (mine if j == 0 else mine + 1 - 2 * (mine % 2))
                    hit = jnp.sum(jnp.where(at, member, 0.0), axis=1, keepdims=True)
                    place = jnp.sum(jnp.where(at, rank, 0.0), axis=1, keepdims=True)
                    onehot = jnp.where((place == slot) & (hit > 0.5), 1.0, 0.0).astype(BF16)
                    placing[i, :, j * cap : (j + 1) * cap] = onehot
                    column = (j * step + local) * cap
                    wide[local * rows : (local + 1) * rows, column : column + cap] = onehot
            onehot = wide[...]
            to = slice(begin * cap, (begin + step) * cap)

            def rows_of(parts):
                got = lax.dot_general(
                    onehot,
                    jnp.concatenate(parts, axis=0),
                    (((0,), (0,)), ((), ())),
                    preferred_element_type=F32,
                ).astype(BF16)
                return got[: step * cap], got[step * cap :]

            these = ins[begin : begin + step]
            near[to, :SHARED], other[to, :SHARED] = rows_of([r[:, :SHARED] for r in these])
            near[to, own], other[to, own] = rows_of([r[:, SHARED:edge] for r in these])
            near[to, theirs], other[to, theirs] = rows_of(pieces[begin : begin + step])
            meta[to, :], other[to, features:] = rows_of([r[:, edge:] for r in these])

    shape = lambda *s: jax.ShapeDtypeStruct(s, BF16)
    return call(
        body,
        (
            shape(count * cap, features),
            shape(count * cap, LANES),
            shape(count * cap, features + LANES),
            shape(count, rows, 2 * cap),
        ),
        4 * count * cap * rows * features,
        2 * count * (rows + 2 * cap) * features,
        20,
        in_specs=[SMEM] + [pl.BlockSpec(memory_space=pltpu.HBM)] * total,
        out_specs=(VMEM,) * 4,
        scratch_shapes=[pltpu.VMEM((step * rows, 2 * step * cap), BF16)]
        + [pltpu.VMEM(a.shape, BF16) for a in (*blocks, *more)]
        + [pltpu.SemaphoreType.DMA((total,))],
    )(jnp.stack([me, at_x]), *blocks, *more)


def mix(placing, near, far, far_first, first, count, at_x, late, adds=(), dtype=BF16):
    _, rows, both = placing.shape
    cap = both // 2
    half = near.shape[1] // 2
    rest = half - OVER_X
    width = OVER_X if late else half + rest

    def body(x_ref, placing, near, far, *refs):
        out = refs[-1]
        own = pl.multiple_of(x_ref[0] * half, LANES)
        other = pl.multiple_of((1 - x_ref[0]) * half, LANES)
        if late:
            parts = [(other, OVER_X, 0)]
        else:
            parts = [
                (own, OVER_X, 0),
                (pl.multiple_of(own + OVER_X, LANES), rest, OVER_X),
                (pl.multiple_of(other + OVER_X, LANES), rest, half),
            ]
        for start, size, to in parts:
            columns = pl.ds(start, size)
            slots = jnp.concatenate([near[:, columns], far[:, columns]], axis=0)
            total = jnp.dot(placing[0], slots, preferred_element_type=F32)
            for ref in refs[:-1]:
                if to + size <= ref.shape[1]:
                    total = total + ref[:, to : to + size].astype(F32)
            out[:, to : to + size] = total.astype(dtype)

    def at(base):
        return lambda g: (g + base, 0)

    return call(
        body,
        jax.ShapeDtypeStruct((count * rows, width), dtype),
        4 * count * rows * cap * width,
        2 * count * (rows + 2 * cap) * width,
        12,
        grid=(count,),
        in_specs=[
            SMEM,
            pl.BlockSpec((1, rows, both), lambda g: (g + first, 0, 0)),
            pl.BlockSpec((cap, 2 * half), at(first)),
            pl.BlockSpec((cap, 2 * half), at(first - far_first)),
        ]
        + [pl.BlockSpec((rows, a.shape[1]), at(base)) for a, base in adds],
        out_specs=pl.BlockSpec((rows, width), at(0)),
    )(at_x.reshape(1), placing, near, far, *[a for a, _ in adds])


def attend_pair(q_input, k_input, v_input, docs, past, at_x):
    rows, width = q_input.shape
    scale = HD ** (-0.5)
    turn = (((1,), (1,)), ((), ()))

    def body(x_ref, q, k, v, docs, past_k, past_v, past_docs, out, bias):
        @pl.when(pl.program_id(0) == 0)
        def _():
            i = lax.broadcasted_iota(jnp.int32, (rows, rows), 0)
            j = lax.broadcasted_iota(jnp.int32, (rows, rows), 1)
            same = lax.dot_general(docs[...], past_docs[...], turn, preferred_element_type=F32)
            bias[:, :rows] = jnp.where((same > 0.5) & (x_ref[0] > 0), 0.0, -1e30)
            same = lax.dot_general(docs[...], docs[...], turn, preferred_element_type=F32)
            bias[:, rows:] = jnp.where((same > 0.5) & (j <= i), 0.0, -1e30)

        query = q[...]
        early = lax.dot_general(query, past_k[...], turn, preferred_element_type=F32)
        late = lax.dot_general(query, k[...], turn, preferred_element_type=F32)
        early = early * scale + bias[:, :rows]
        late = late * scale + bias[:, rows:]
        top = jnp.maximum(
            jnp.max(early, axis=1, keepdims=True), jnp.max(late, axis=1, keepdims=True)
        )
        early, late = jnp.exp(early - top), jnp.exp(late - top)
        total = jnp.sum(early, axis=1, keepdims=True) + jnp.sum(late, axis=1, keepdims=True)
        mixed = jnp.dot(early.astype(BF16), past_v[...], preferred_element_type=F32) + jnp.dot(
            late.astype(BF16), v[...], preferred_element_type=F32
        )
        out[...] = (mixed / total).astype(BF16)

    heads = width // HD
    head = pl.BlockSpec((rows, HD), lambda h: (0, h))
    return call(
        body,
        jax.ShapeDtypeStruct((rows, width), BF16),
        8 * rows * rows * width,
        14 * rows * width,
        14,
        grid=(heads,),
        in_specs=[
            SMEM,
            head,
            head,
            head,
            pl.BlockSpec((rows, LANES), lambda h: (0, 0)),
            head,
            pl.BlockSpec((rows, HD), lambda h: (0, heads + h)),
            pl.BlockSpec((rows, LANES), lambda h: (0, 2 * heads)),
        ],
        out_specs=head,
        scratch_shapes=[pltpu.VMEM((rows, 2 * rows), F32)],
    )(at_x.reshape(1), q_input, k_input, v_input, docs, past, past, past)


def spread(onehot):
    blocks, cap, rows = onehot.shape
    same = jnp.eye(blocks, dtype=jnp.bool_)
    wide = onehot[:, :, None, :] & same[:, None, :, None]
    return wide.reshape(blocks * cap, blocks * rows).astype(BF16)


def solution(mesh):
    n_ctx = mesh.shape["ctx"]
    n_exp = mesh.shape["exp"]
    nz = n_exp // 4

    def pairs(move):
        out = []
        for i in range(n_exp):
            z, y, c = i // 4, (i // 2) % 2, i % 2
            z, y, c = move(z, y, c)
            out.append((i, (z % nz * 2 + y) * 2 + c))
        return out

    def z_shift(x, d):
        return lax.ppermute(x, "exp", pairs(lambda z, y, c: (z + d, y, c)))

    def y_swap(x):
        return lax.ppermute(x, "exp", pairs(lambda z, y, c: (z, 1 - y, c)))

    def core_swap(x):
        return lax.ppermute(x, "exp", pairs(lambda z, y, c: (z, y, 1 - c)))

    def x_swap(x):
        return lax.ppermute(x, "ctx", [(0, 1), (1, 0)])

    def on_device(
        q_input, k_input, v_input, segment_ids, tokens, expert_ids, route_weight, w_in, w_down
    ):
        me = lax.axis_index("exp")
        at_x = lax.axis_index("ctx")
        rows, width = tokens.shape
        cap = rows * 8 // n_exp
        half = width // 2
        near = n_exp // 2
        slots = near * cap

        if n_ctx == 2:
            plan = [("x", 1024), ("x", 1024), ("", 1024), ("x", 1024), ("", 1024)]
        else:
            plan = [("", width)]
        arrived = []
        start = 0
        for kind, size in plan:
            if kind == "x":
                block = lax.dynamic_slice_in_dim(tokens, start + at_x * (size // 2), size // 2, 1)
            else:
                block = tokens[:, start : start + size]
            line = jnp.concatenate([block] + [z_shift(block, d) for d in range(1, nz)], axis=0)
            both = jnp.concatenate([line, y_swap(line)], axis=0)
            if kind == "x":
                other = x_swap(both)
                both = jnp.concatenate(
                    [jnp.where(at_x == 0, both, other), jnp.where(at_x == 0, other, both)], axis=1
                )
            arrived.append((start, size, both))
            start += size

        meta = jnp.concatenate([expert_ids.astype(F32), route_weight], axis=1)
        meta = lax.all_gather(meta, "exp", axis=0, tiled=False)
        z, y, c = me // 4, (me // 2) % 2, me % 2
        order = jnp.stack(
            [
                ((z - d + nz) % nz * 2 + (y + yr) % 2) * 2 + (c + cr) % 2
                for cr in range(2)
                for yr in range(2)
                for d in range(nz)
            ]
        )
        meta = meta[order]
        ids, weights = meta[:, :, :TOP].astype(jnp.int32), meta[:, :, TOP:]

        def placing(ids, expert):
            named = ids == expert
            hit = jnp.any(named, axis=2)
            count = hit.astype(jnp.int32)
            rank = jnp.cumsum(count, axis=1) - count
            slot = jnp.arange(cap, dtype=jnp.int32)
            return named, hit[:, None, :] & (rank[:, None, :] == slot[None, :, None])

        named, mine = placing(ids, me)
        _, others = placing(ids[:near], me + 1 - 2 * c)
        weight = jnp.sum(jnp.where(named, weights, 0.0), axis=2)
        weight = jnp.sum(jnp.where(mine, weight[:, None, :], 0.0), axis=2).reshape(2 * slots, 1)
        place = jnp.concatenate([spread(mine[:near]), spread(others)], axis=0)

        gate = up = None
        for start, size, both in arrived:
            placed = jnp.dot(place, both, preferred_element_type=F32).astype(BF16)
            block = jnp.concatenate([placed[:slots], core_swap(placed[slots:])], axis=0)
            g = jnp.dot(block, w_in[0, 0, start : start + size], preferred_element_type=F32)
            u = jnp.dot(block, w_in[0, 1, start : start + size], preferred_element_type=F32)
            gate = g if gate is None else gate + g
            up = u if up is None else up + u
        hidden = (jax.nn.silu(gate) * up).astype(BF16)

        if n_ctx == 2:
            back = [("x", 512), ("x", 512), ("", 512), ("x", 512), ("", 512)]
        else:
            back = [("", half)]
        down = w_down[0]
        pieces = []
        start = 0
        for kind, size in back:
            if n_ctx == 2:
                cols = jnp.concatenate(
                    [down[:, start : start + size], down[:, half + start : half + start + size]],
                    axis=1,
                )
            else:
                cols = down
            part = jnp.dot(hidden, cols, preferred_element_type=F32)
            part = (part * weight).astype(BF16)
            part = jnp.concatenate([part[:slots], core_swap(part[slots:])], axis=0)
            summed = lax.dot_general(
                place, part, (((0,), (0,)), ((), ())), preferred_element_type=F32
            )

            def over_x(summed):
                first, second = summed[:, :size].astype(BF16), summed[:, size:].astype(BF16)
                other = x_swap(jnp.where(at_x == 0, second, first))
                own = jnp.where(at_x == 0, summed[:, :size], summed[:, size:])
                return own + other.astype(F32)

            if kind == "x":
                summed = over_x(summed)
            count = nz * rows
            summed = summed[:count] + y_swap(summed[count:].astype(BF16)).astype(F32)
            total = summed[:rows]
            for d in range(1, nz):
                block = summed[d * rows : (d + 1) * rows].astype(BF16)
                total = total + z_shift(block, -d).astype(F32)
            if kind != "x":
                if n_ctx == 2:
                    total = over_x(total)
                else:
                    total = lax.psum_scatter(
                        total.astype(BF16), "ctx", scatter_dimension=1, tiled=True
                    )
            pieces.append(total.astype(BF16))
            start += size
        moe_out = jnp.concatenate(pieces, axis=1)
        attn_out = attend(q_input, k_input, v_input, segment_ids, n_ctx)
        return attn_out, moe_out

    def pair_device(
        q_input, k_input, v_input, segment_ids, tokens, expert_ids, route_weight, w_in, w_down
    ):
        me = lax.axis_index("exp")
        at_x = lax.axis_index("ctx")
        rows, width = tokens.shape
        cap = rows * 8 // n_exp
        half = width // 2
        split = (width - SHARED) // 2
        after = lax.optimization_barrier

        block, theirs = prepare(tokens, expert_ids, route_weight, at_x, n_exp)
        cut = lambda a: a[:, SHARED : SHARED + split]
        both = lambda d: jnp.concatenate([cut(line[d]), cut(across[d])], axis=0)
        line = {0: block, 1: z_shift(block, 1), 3: z_shift(block, -1)}
        line[2] = z_shift(line[1], 1)
        across = {0: y_swap(block)}
        block, segment_ids, k_input = after((block, segment_ids, k_input))
        docs = segment_ids[:, None] == jnp.arange(LANES, dtype=jnp.int32)
        docs = docs.astype(BF16)
        past = lax.ppermute(jnp.concatenate([k_input, v_input, docs], axis=1), "ctx", [(0, 1)])
        line[1], across[0] = after((line[1], across[0]))
        across[1] = y_swap(line[1])
        line[3], across[1] = after((line[3], across[1]))
        across[3] = y_swap(line[3])
        across[0], past = after((across[0], past))
        more = {0: [theirs, x_swap(cut(across[0]))], 1: [x_swap(both(1))]}
        line[2], across[3], before = after((line[2], across[3], more[0][1]))
        more[0][1] = before
        across[2] = y_swap(line[2])
        more[3] = [x_swap(both(3))]
        line[2], before = after((line[2], more[1][0]))
        more[1] = [before]
        more[2] = [x_swap(cut(line[2]))]
        attn_out = attend_pair(q_input, k_input, v_input, docs, past, at_x)
        across[2], before, attn_out = after((across[2], more[3][0], attn_out))
        more[3] = [before]
        more[2].append(x_swap(cut(across[2])))

        near, meta, sent, placing = pick(
            [b for d in ORDER for b in (line[d], across[d])],
            [a for d in ORDER for a in more[d]],
            me,
            at_x,
            cap,
        )
        far = core_swap(sent)
        def expert(block, meta):
            gate = jnp.dot(block, w_in[0, 0], preferred_element_type=F32)
            up = jnp.dot(block, w_in[0, 1], preferred_element_type=F32)
            gate, up = after((gate, up))
            hidden = (jax.nn.silu(gate) * up).astype(BF16)
            lane = jnp.arange(LANES, dtype=jnp.int32)
            at = (lane % n_exp == me) & (lane >= n_exp) & (lane < 4 * n_exp)
            scale = jnp.sum(jnp.where(at, meta.astype(F32), 0.0), axis=1, keepdims=True)
            hidden, scale = after((hidden, scale))
            out = jnp.dot(hidden, w_down[0], preferred_element_type=F32)
            return (out * scale).astype(BF16)

        near = expert(near, meta)
        near, far = after((near, far))
        sent = expert(far[:, :width], far[:, width:])
        edge = sent.shape[0] // 2
        far_a = core_swap(sent[:edge])
        far_a, rest = after((far_a, sent[edge:]))
        far_b = core_swap(rest)

        def sums(i, count, late, adds=(), dtype=BF16):
            far, begin = (far_a, 0) if i < 4 else (far_b, 4)
            return mix(placing, near, far, begin, i, count, at_x, late, adds, dtype)

        got_x = []
        for i in range(4):
            late = sums(2 * i, 2, True)
            near, late = after((near, late))
            got_x.append(x_swap(late))

        def over_y(i):
            return y_swap(sums(2 * i + 1, 1, False, [(got_x[i], 1)]))

        got_y = [over_y(0), over_y(1)]
        part = sums(0, 1, False, [(got_x[0], 0), (got_y[0], 0)])
        part = z_shift(part, -1)
        got_x[2], part = after((got_x[2], part))
        got_y.append(over_y(2))
        part = sums(2, 1, False, [(got_x[1], 0), (got_y[1], 0), (part, 0)])
        right = z_shift(part, -1)
        got_x[3], right = after((got_x[3], right))
        got_y.append(over_y(3))
        left = z_shift(sums(4, 1, False, [(got_x[2], 0), (got_y[2], 0)]), 1)
        total = sums(6, 1, False, [(got_x[3], 0), (got_y[3], 0)], F32)
        total = total + right.astype(F32) + left.astype(F32)
        got = x_swap(total[:, half:].astype(BF16))
        moe_out = jnp.concatenate(
            [total[:, :OVER_X], total[:, OVER_X:half] + got.astype(F32)], axis=1
        ).astype(BF16)
        return attn_out, moe_out

    in_specs = (
        P("ctx", "exp"),
        P("ctx", "exp"),
        P("ctx", "exp"),
        P("ctx"),
        P("exp", None),
        P("exp", None),
        P("exp", None),
        P("exp", None, None, "ctx"),
        P("exp", "ctx", None),
    )
    out_specs = (P("ctx", "exp"), P("exp", "ctx"))
    return jax.shard_map(
        pair_device if n_ctx == 2 and nz == 4 else on_device,
        mesh=mesh,
        in_specs=in_specs,
        out_specs=out_specs,
        check_vma=False,
    )
```

```python
import jax
import jax.numpy as jnp
from jax import lax
from jax.experimental import pallas as pl
from jax.experimental.pallas import tpu as pltpu
from jax.sharding import PartitionSpec as P

HD = 128
TOP = 6
BF16 = jnp.bfloat16
F32 = jnp.float32


def attend(q_input, k_input, v_input, segment_ids, n_ctx):
    scale = HD ** (-0.5)
    rows = q_input.shape[0]
    heads = q_input.shape[1] // HD
    place = lax.axis_index("ctx") * rows + jnp.arange(rows, dtype=jnp.int32)
    if n_ctx == 2:
        ahead = [(0, 1)]
        keys = jnp.concatenate([lax.ppermute(k_input, "ctx", ahead), k_input], axis=0)
        values = jnp.concatenate([lax.ppermute(v_input, "ctx", ahead), v_input], axis=0)
        docs = jnp.concatenate([lax.ppermute(segment_ids, "ctx", ahead), segment_ids], axis=0)
        first = (lax.axis_index("ctx") - 1) * rows
    else:
        keys = lax.all_gather(k_input, "ctx", axis=0, tiled=True)
        values = lax.all_gather(v_input, "ctx", axis=0, tiled=True)
        docs = lax.all_gather(segment_ids, "ctx", axis=0, tiled=True)
        first = 0
    count = keys.shape[0]
    key_place = first + jnp.arange(count, dtype=jnp.int32)
    visible = (
        (key_place[None, :] <= place[:, None])
        & (key_place[None, :] >= 0)
        & (docs[None, :] == segment_ids[:, None])
    )
    queries = q_input.reshape(rows, heads, HD)
    scores = (
        jnp.einsum(
            "qhd,khd->qhk", queries, keys.reshape(count, heads, HD), preferred_element_type=F32
        )
        * scale
    )
    scores = jnp.where(visible[:, None, :], scores, -1e30)
    newest = jnp.max(scores, axis=2)
    probs = jnp.where(visible[:, None, :], jnp.exp(scores - newest[:, :, None]), 0.0)
    total = jnp.sum(probs, axis=2)
    summed = jnp.einsum(
        "qhk,khd->qhd",
        probs.astype(BF16),
        values.reshape(count, heads, HD),
        preferred_element_type=F32,
    )
    return (summed / total[:, :, None]).reshape(rows, heads * HD).astype(BF16)

SHARED = 2560
OVER_X = 1536
ORDER = [2, 1, 3, 0]

VMEM = pl.BlockSpec(memory_space=pltpu.VMEM)
SMEM = pl.BlockSpec(memory_space=pltpu.SMEM)
MIB = 1024 * 1024
LANES = 128


def call(body, out_shape, flops, moved, room, **kw):
    return pl.pallas_call(
        body,
        out_shape=out_shape,
        compiler_params=pltpu.CompilerParams(vmem_limit_bytes=room * MIB),
        cost_estimate=pl.CostEstimate(flops=flops, bytes_accessed=moved, transcendentals=0),
        **kw,
    )


def prepare(tokens, expert_ids, route_weight, at_x, experts):
    rows, width = tokens.shape
    split = (width - SHARED) // 2

    def body(x_ref, tokens, ids, weights, out, theirs):
        own = pl.ds(pl.multiple_of(SHARED + x_ref[0] * split, LANES), split)
        other = pl.ds(pl.multiple_of(SHARED + (1 - x_ref[0]) * split, LANES), split)
        out[:, :SHARED] = tokens[:, :SHARED]
        out[:, SHARED : SHARED + split] = tokens[:, own]
        theirs[...] = tokens[:, other]
        column = lax.broadcasted_iota(jnp.int32, (LANES, rows), 0)
        expert, term = column % experts, column // experts
        meta = jnp.zeros((LANES, rows), F32)
        for k in range(TOP):
            weight = jnp.broadcast_to(weights[k : k + 1, :], (LANES, rows))
            high = weight.astype(BF16).astype(F32)
            middle = (weight - high).astype(BF16).astype(F32)
            low = weight - high - middle
            value = jnp.where(term == 1, high, jnp.where(term == 2, middle, low))
            value = jnp.where(term == 0, 1.0, value)
            meta = jnp.where((ids[k : k + 1, :] == expert) & (term < 4), value, meta)
        eye = lax.broadcasted_iota(jnp.int32, (LANES, LANES), 0) == lax.broadcasted_iota(
            jnp.int32, (LANES, LANES), 1
        )
        meta = lax.dot_general(
            meta.astype(BF16),
            jnp.where(eye, 1.0, 0.0).astype(BF16),
            (((0,), (0,)), ((), ())),
            preferred_element_type=F32,
        )
        out[:, SHARED + split :] = meta.astype(BF16)

    return call(
        body,
        (
            jax.ShapeDtypeStruct((rows, SHARED + split + LANES), BF16),
            jax.ShapeDtypeStruct((rows, split), BF16),
        ),
        0,
        4 * rows * width,
        8,
        in_specs=[SMEM] + [VMEM] * 3,
        out_specs=(VMEM,) * 2,
    )(at_x.reshape(1), tokens, expert_ids.T, route_weight.T)


def pick(blocks, more, me, at_x, cap):
    count = len(blocks)
    rows, width = blocks[0].shape
    split = more[0].shape[1]
    edge = width - LANES
    features = edge + split
    step = 4
    total = count + len(more)

    def body(s_ref, *refs):
        sources, (near, meta, other, placing, wide, *held, done) = refs[:total], refs[total:]
        copies = [
            pltpu.make_async_copy(source, to, done.at[i])
            for i, (source, to) in enumerate(zip(sources, held))
        ]
        for copy in copies:
            copy.start()
        for copy in copies:
            copy.wait()
        ins, extra = held[:count], held[count:]
        mine, x = s_ref[0], s_ref[1]
        lane = lax.broadcasted_iota(jnp.int32, (rows, LANES), 1)
        earlier = lax.broadcasted_iota(jnp.int32, (rows, rows), 0) > lax.broadcasted_iota(
            jnp.int32, (rows, rows), 1
        )
        slot = lax.broadcasted_iota(jnp.int32, (rows, cap), 1).astype(F32)
        own = pl.ds(pl.multiple_of(SHARED + x * split, LANES), split)
        theirs = pl.ds(pl.multiple_of(SHARED + (1 - x) * split, LANES), split)
        pieces = [
            ref[b * rows : (b + 1) * rows, :] for ref in extra for b in range(ref.shape[0] // rows)
        ]
        for begin in range(0, count, step):
            wide[...] = jnp.zeros_like(wide)
            for i in range(begin, begin + step):
                member = ins[i][:, edge:]
                rank = jnp.dot(earlier.astype(BF16), member, preferred_element_type=F32)
                member = member.astype(F32)
                local = i - begin
                for j in range(2):
                    at = lane == (mine if j == 0 else mine + 1 - 2 * (mine % 2))
                    hit = jnp.sum(jnp.where(at, member, 0.0), axis=1, keepdims=True)
                    place = jnp.sum(jnp.where(at, rank, 0.0), axis=1, keepdims=True)
                    onehot = jnp.where((place == slot) & (hit > 0.5), 1.0, 0.0).astype(BF16)
                    placing[i, :, j * cap : (j + 1) * cap] = onehot
                    column = (j * step + local) * cap
                    wide[local * rows : (local + 1) * rows, column : column + cap] = onehot
            onehot = wide[...]
            to = slice(begin * cap, (begin + step) * cap)

            def rows_of(parts):
                got = lax.dot_general(
                    onehot,
                    jnp.concatenate(parts, axis=0),
                    (((0,), (0,)), ((), ())),
                    preferred_element_type=F32,
                ).astype(BF16)
                return got[: step * cap], got[step * cap :]

            these = ins[begin : begin + step]
            near[to, :SHARED], other[to, :SHARED] = rows_of([r[:, :SHARED] for r in these])
            near[to, own], other[to, own] = rows_of([r[:, SHARED:edge] for r in these])
            near[to, theirs], other[to, theirs] = rows_of(pieces[begin : begin + step])
            meta[to, :], other[to, features:] = rows_of([r[:, edge:] for r in these])

    shape = lambda *s: jax.ShapeDtypeStruct(s, BF16)
    return call(
        body,
        (
            shape(count * cap, features),
            shape(count * cap, LANES),
            shape(count * cap, features + LANES),
            shape(count, rows, 2 * cap),
        ),
        4 * count * cap * rows * features,
        2 * count * (rows + 2 * cap) * features,
        20,
        in_specs=[SMEM] + [pl.BlockSpec(memory_space=pltpu.HBM)] * total,
        out_specs=(VMEM,) * 4,
        scratch_shapes=[pltpu.VMEM((step * rows, 2 * step * cap), BF16)]
        + [pltpu.VMEM(a.shape, BF16) for a in (*blocks, *more)]
        + [pltpu.SemaphoreType.DMA((total,))],
    )(jnp.stack([me, at_x]), *blocks, *more)


def mix(placing, near, far, far_first, first, count, at_x, late, adds=(), dtype=BF16):
    _, rows, both = placing.shape
    cap = both // 2
    half = near.shape[1] // 2
    rest = half - OVER_X
    width = OVER_X if late else half + rest

    def body(x_ref, placing, near, far, *refs):
        out = refs[-1]
        own = pl.multiple_of(x_ref[0] * half, LANES)
        other = pl.multiple_of((1 - x_ref[0]) * half, LANES)
        if late:
            parts = [(other, OVER_X, 0)]
        else:
            parts = [
                (own, OVER_X, 0),
                (pl.multiple_of(own + OVER_X, LANES), rest, OVER_X),
                (pl.multiple_of(other + OVER_X, LANES), rest, half),
            ]
        for start, size, to in parts:
            columns = pl.ds(start, size)
            slots = jnp.concatenate([near[:, columns], far[:, columns]], axis=0)
            total = jnp.dot(placing[0], slots, preferred_element_type=F32)
            for ref in refs[:-1]:
                if to + size <= ref.shape[1]:
                    total = total + ref[:, to : to + size].astype(F32)
            out[:, to : to + size] = total.astype(dtype)

    def at(base):
        return lambda g: (g + base, 0)

    return call(
        body,
        jax.ShapeDtypeStruct((count * rows, width), dtype),
        4 * count * rows * cap * width,
        2 * count * (rows + 2 * cap) * width,
        12,
        grid=(count,),
        in_specs=[
            SMEM,
            pl.BlockSpec((1, rows, both), lambda g: (g + first, 0, 0)),
            pl.BlockSpec((cap, 2 * half), at(first)),
            pl.BlockSpec((cap, 2 * half), at(first - far_first)),
        ]
        + [pl.BlockSpec((rows, a.shape[1]), at(base)) for a, base in adds],
        out_specs=pl.BlockSpec((rows, width), at(0)),
    )(at_x.reshape(1), placing, near, far, *[a for a, _ in adds])


def attend_pair(q_input, k_input, v_input, docs, past, at_x):
    rows, width = q_input.shape
    scale = HD ** (-0.5)
    turn = (((1,), (1,)), ((), ()))

    def body(x_ref, q, k, v, docs, past_k, past_v, past_docs, out, bias):
        @pl.when(pl.program_id(0) == 0)
        def _():
            i = lax.broadcasted_iota(jnp.int32, (rows, rows), 0)
            j = lax.broadcasted_iota(jnp.int32, (rows, rows), 1)
            same = lax.dot_general(docs[...], past_docs[...], turn, preferred_element_type=F32)
            bias[:, :rows] = jnp.where((same > 0.5) & (x_ref[0] > 0), 0.0, -1e30)
            same = lax.dot_general(docs[...], docs[...], turn, preferred_element_type=F32)
            bias[:, rows:] = jnp.where((same > 0.5) & (j <= i), 0.0, -1e30)

        query = q[...]
        early = lax.dot_general(query, past_k[...], turn, preferred_element_type=F32)
        late = lax.dot_general(query, k[...], turn, preferred_element_type=F32)
        early = early * scale + bias[:, :rows]
        late = late * scale + bias[:, rows:]
        top = jnp.maximum(
            jnp.max(early, axis=1, keepdims=True), jnp.max(late, axis=1, keepdims=True)
        )
        early, late = jnp.exp(early - top), jnp.exp(late - top)
        total = jnp.sum(early, axis=1, keepdims=True) + jnp.sum(late, axis=1, keepdims=True)
        mixed = jnp.dot(early.astype(BF16), past_v[...], preferred_element_type=F32) + jnp.dot(
            late.astype(BF16), v[...], preferred_element_type=F32
        )
        out[...] = (mixed / total).astype(BF16)

    heads = width // HD
    head = pl.BlockSpec((rows, HD), lambda h: (0, h))
    return call(
        body,
        jax.ShapeDtypeStruct((rows, width), BF16),
        8 * rows * rows * width,
        14 * rows * width,
        14,
        grid=(heads,),
        in_specs=[
            SMEM,
            head,
            head,
            head,
            pl.BlockSpec((rows, LANES), lambda h: (0, 0)),
            head,
            pl.BlockSpec((rows, HD), lambda h: (0, heads + h)),
            pl.BlockSpec((rows, LANES), lambda h: (0, 2 * heads)),
        ],
        out_specs=head,
        scratch_shapes=[pltpu.VMEM((rows, 2 * rows), F32)],
    )(at_x.reshape(1), q_input, k_input, v_input, docs, past, past, past)


def spread(onehot):
    blocks, cap, rows = onehot.shape
    same = jnp.eye(blocks, dtype=jnp.bool_)
    wide = onehot[:, :, None, :] & same[:, None, :, None]
    return wide.reshape(blocks * cap, blocks * rows).astype(BF16)


def solution(mesh):
    n_ctx = mesh.shape["ctx"]
    n_exp = mesh.shape["exp"]
    nz = n_exp // 4

    def pairs(move):
        out = []
        for i in range(n_exp):
            z, y, c = i // 4, (i // 2) % 2, i % 2
            z, y, c = move(z, y, c)
            out.append((i, (z % nz * 2 + y) * 2 + c))
        return out

    def z_shift(x, d):
        return lax.ppermute(x, "exp", pairs(lambda z, y, c: (z + d, y, c)))

    def y_swap(x):
        return lax.ppermute(x, "exp", pairs(lambda z, y, c: (z, 1 - y, c)))

    def core_swap(x):
        return lax.ppermute(x, "exp", pairs(lambda z, y, c: (z, y, 1 - c)))

    def x_swap(x):
        return lax.ppermute(x, "ctx", [(0, 1), (1, 0)])

    def on_device(
        q_input, k_input, v_input, segment_ids, tokens, expert_ids, route_weight, w_in, w_down
    ):
        me = lax.axis_index("exp")
        at_x = lax.axis_index("ctx")
        rows, width = tokens.shape
        cap = rows * 8 // n_exp
        half = width // 2
        near = n_exp // 2
        slots = near * cap

        if n_ctx == 2:
            plan = [("x", 1024), ("x", 1024), ("", 1024), ("x", 1024), ("", 1024)]
        else:
            plan = [("", width)]
        arrived = []
        start = 0
        for kind, size in plan:
            if kind == "x":
                block = lax.dynamic_slice_in_dim(tokens, start + at_x * (size // 2), size // 2, 1)
            else:
                block = tokens[:, start : start + size]
            line = jnp.concatenate([block] + [z_shift(block, d) for d in range(1, nz)], axis=0)
            both = jnp.concatenate([line, y_swap(line)], axis=0)
            if kind == "x":
                other = x_swap(both)
                both = jnp.concatenate(
                    [jnp.where(at_x == 0, both, other), jnp.where(at_x == 0, other, both)], axis=1
                )
            arrived.append((start, size, both))
            start += size

        meta = jnp.concatenate([expert_ids.astype(F32), route_weight], axis=1)
        meta = lax.all_gather(meta, "exp", axis=0, tiled=False)
        z, y, c = me // 4, (me // 2) % 2, me % 2
        order = jnp.stack(
            [
                ((z - d + nz) % nz * 2 + (y + yr) % 2) * 2 + (c + cr) % 2
                for cr in range(2)
                for yr in range(2)
                for d in range(nz)
            ]
        )
        meta = meta[order]
        ids, weights = meta[:, :, :TOP].astype(jnp.int32), meta[:, :, TOP:]

        def placing(ids, expert):
            named = ids == expert
            hit = jnp.any(named, axis=2)
            count = hit.astype(jnp.int32)
            rank = jnp.cumsum(count, axis=1) - count
            slot = jnp.arange(cap, dtype=jnp.int32)
            return named, hit[:, None, :] & (rank[:, None, :] == slot[None, :, None])

        named, mine = placing(ids, me)
        _, others = placing(ids[:near], me + 1 - 2 * c)
        weight = jnp.sum(jnp.where(named, weights, 0.0), axis=2)
        weight = jnp.sum(jnp.where(mine, weight[:, None, :], 0.0), axis=2).reshape(2 * slots, 1)
        place = jnp.concatenate([spread(mine[:near]), spread(others)], axis=0)

        gate = up = None
        for start, size, both in arrived:
            placed = jnp.dot(place, both, preferred_element_type=F32).astype(BF16)
            block = jnp.concatenate([placed[:slots], core_swap(placed[slots:])], axis=0)
            g = jnp.dot(block, w_in[0, 0, start : start + size], preferred_element_type=F32)
            u = jnp.dot(block, w_in[0, 1, start : start + size], preferred_element_type=F32)
            gate = g if gate is None else gate + g
            up = u if up is None else up + u
        hidden = (jax.nn.silu(gate) * up).astype(BF16)

        if n_ctx == 2:
            back = [("x", 512), ("x", 512), ("", 512), ("x", 512), ("", 512)]
        else:
            back = [("", half)]
        down = w_down[0]
        pieces = []
        start = 0
        for kind, size in back:
            if n_ctx == 2:
                cols = jnp.concatenate(
                    [down[:, start : start + size], down[:, half + start : half + start + size]],
                    axis=1,
                )
            else:
                cols = down
            part = jnp.dot(hidden, cols, preferred_element_type=F32)
            part = (part * weight).astype(BF16)
            part = jnp.concatenate([part[:slots], core_swap(part[slots:])], axis=0)
            summed = lax.dot_general(
                place, part, (((0,), (0,)), ((), ())), preferred_element_type=F32
            )

            def over_x(summed):
                first, second = summed[:, :size].astype(BF16), summed[:, size:].astype(BF16)
                other = x_swap(jnp.where(at_x == 0, second, first))
                own = jnp.where(at_x == 0, summed[:, :size], summed[:, size:])
                return own + other.astype(F32)

            if kind == "x":
                summed = over_x(summed)
            count = nz * rows
            summed = summed[:count] + y_swap(summed[count:].astype(BF16)).astype(F32)
            total = summed[:rows]
            for d in range(1, nz):
                block = summed[d * rows : (d + 1) * rows].astype(BF16)
                total = total + z_shift(block, -d).astype(F32)
            if kind != "x":
                if n_ctx == 2:
                    total = over_x(total)
                else:
                    total = lax.psum_scatter(
                        total.astype(BF16), "ctx", scatter_dimension=1, tiled=True
                    )
            pieces.append(total.astype(BF16))
            start += size
        moe_out = jnp.concatenate(pieces, axis=1)
        attn_out = attend(q_input, k_input, v_input, segment_ids, n_ctx)
        return attn_out, moe_out

    def pair_device(
        q_input, k_input, v_input, segment_ids, tokens, expert_ids, route_weight, w_in, w_down
    ):
        me = lax.axis_index("exp")
        at_x = lax.axis_index("ctx")
        rows, width = tokens.shape
        cap = rows * 8 // n_exp
        half = width // 2
        split = (width - SHARED) // 2
        after = lax.optimization_barrier

        block, theirs = prepare(tokens, expert_ids, route_weight, at_x, n_exp)
        cut = lambda a: a[:, SHARED : SHARED + split]
        both = lambda d: jnp.concatenate([cut(line[d]), cut(across[d])], axis=0)
        line = {0: block, 1: z_shift(block, 1)}
        across = {0: y_swap(block)}
        line[1], again = after((line[1], block))
        line[3] = z_shift(again, -1)
        line[3], again = after((line[3], line[1]))
        line[2] = z_shift(again, 1)
        block, segment_ids, k_input = after((block, segment_ids, k_input))
        docs = segment_ids[:, None] == jnp.arange(LANES, dtype=jnp.int32)
        docs = docs.astype(BF16)
        past = lax.ppermute(jnp.concatenate([k_input, v_input, docs], axis=1), "ctx", [(0, 1)])
        line[1], across[0] = after((line[1], across[0]))
        across[1] = y_swap(line[1])
        line[3], across[1] = after((line[3], across[1]))
        across[3] = y_swap(line[3])
        across[0], past = after((across[0], past))
        more = {0: [theirs, x_swap(cut(across[0]))], 1: [x_swap(both(1))]}
        line[2], across[3], before = after((line[2], across[3], more[0][1]))
        more[0][1] = before
        across[2] = y_swap(line[2])
        more[3] = [x_swap(both(3))]
        line[2], before = after((line[2], more[1][0]))
        more[1] = [before]
        more[2] = [x_swap(cut(line[2]))]
        attn_out = attend_pair(q_input, k_input, v_input, docs, past, at_x)
        across[2], before, attn_out = after((across[2], more[3][0], attn_out))
        more[3] = [before]
        more[2].append(x_swap(cut(across[2])))

        near, meta, sent, placing = pick(
            [b for d in ORDER for b in (line[d], across[d])],
            [a for d in ORDER for a in more[d]],
            me,
            at_x,
            cap,
        )
        far = core_swap(sent)
        def expert(block, meta):
            gate = jnp.dot(block, w_in[0, 0], preferred_element_type=F32)
            up = jnp.dot(block, w_in[0, 1], preferred_element_type=F32)
            gate, up = after((gate, up))
            hidden = (jax.nn.silu(gate) * up).astype(BF16)
            lane = jnp.arange(LANES, dtype=jnp.int32)
            at = (lane % n_exp == me) & (lane >= n_exp) & (lane < 4 * n_exp)
            scale = jnp.sum(jnp.where(at, meta.astype(F32), 0.0), axis=1, keepdims=True)
            hidden, scale = after((hidden, scale))
            out = jnp.dot(hidden, w_down[0], preferred_element_type=F32)
            return (out * scale).astype(BF16)

        near = expert(near, meta)
        near, far = after((near, far))
        sent = expert(far[:, :width], far[:, width:])
        edge = sent.shape[0] // 2
        far_a = core_swap(sent[:edge])
        far_a, rest = after((far_a, sent[edge:]))
        far_b = core_swap(rest)

        def sums(i, count, late, adds=(), dtype=BF16):
            far, begin = (far_a, 0) if i < 4 else (far_b, 4)
            return mix(placing, near, far, begin, i, count, at_x, late, adds, dtype)

        got_x = []
        for i in range(4):
            late = sums(2 * i, 2, True)
            near, late = after((near, late))
            got_x.append(x_swap(late))

        def over_y(i):
            return y_swap(sums(2 * i + 1, 1, False, [(got_x[i], 1)]))

        got_y = [over_y(0)]
        turn = sums(3, 1, False, [(got_x[1], 1)])
        got_y[0], turn = after((got_y[0], turn))
        got_y.append(y_swap(turn))
        part = sums(0, 1, False, [(got_x[0], 0), (got_y[0], 0)])
        part = z_shift(part, -1)
        got_x[2], part = after((got_x[2], part))
        got_y.append(over_y(2))
        part = sums(2, 1, False, [(got_x[1], 0), (got_y[1], 0), (part, 0)])
        right = z_shift(part, -1)
        got_x[3], right = after((got_x[3], right))
        got_y.append(over_y(3))
        left = z_shift(sums(4, 1, False, [(got_x[2], 0), (got_y[2], 0)]), 1)
        total = sums(6, 1, False, [(got_x[3], 0), (got_y[3], 0)], F32)
        total = total + right.astype(F32) + left.astype(F32)
        got = x_swap(total[:, half:].astype(BF16))
        moe_out = jnp.concatenate(
            [total[:, :OVER_X], total[:, OVER_X:half] + got.astype(F32)], axis=1
        ).astype(BF16)
        return attn_out, moe_out

    in_specs = (
        P("ctx", "exp"),
        P("ctx", "exp"),
        P("ctx", "exp"),
        P("ctx"),
        P("exp", None),
        P("exp", None),
        P("exp", None),
        P("exp", None, None, "ctx"),
        P("exp", "ctx", None),
    )
    out_specs = (P("ctx", "exp"), P("exp", "ctx"))
    return jax.shard_map(
        pair_device if n_ctx == 2 and nz == 4 else on_device,
        mesh=mesh,
        in_specs=in_specs,
        out_specs=out_specs,
        check_vma=False,
    )
```

```python
import jax
import jax.numpy as jnp
from jax import lax
from jax.experimental import pallas as pl
from jax.experimental.pallas import tpu as pltpu
from jax.sharding import PartitionSpec as P

HD = 128
TOP = 6
BF16 = jnp.bfloat16
F32 = jnp.float32


def attend(q_input, k_input, v_input, segment_ids, n_ctx):
    scale = HD ** (-0.5)
    rows = q_input.shape[0]
    heads = q_input.shape[1] // HD
    place = lax.axis_index("ctx") * rows + jnp.arange(rows, dtype=jnp.int32)
    if n_ctx == 2:
        ahead = [(0, 1)]
        keys = jnp.concatenate([lax.ppermute(k_input, "ctx", ahead), k_input], axis=0)
        values = jnp.concatenate([lax.ppermute(v_input, "ctx", ahead), v_input], axis=0)
        docs = jnp.concatenate([lax.ppermute(segment_ids, "ctx", ahead), segment_ids], axis=0)
        first = (lax.axis_index("ctx") - 1) * rows
    else:
        keys = lax.all_gather(k_input, "ctx", axis=0, tiled=True)
        values = lax.all_gather(v_input, "ctx", axis=0, tiled=True)
        docs = lax.all_gather(segment_ids, "ctx", axis=0, tiled=True)
        first = 0
    count = keys.shape[0]
    key_place = first + jnp.arange(count, dtype=jnp.int32)
    visible = (
        (key_place[None, :] <= place[:, None])
        & (key_place[None, :] >= 0)
        & (docs[None, :] == segment_ids[:, None])
    )
    queries = q_input.reshape(rows, heads, HD)
    scores = (
        jnp.einsum(
            "qhd,khd->qhk", queries, keys.reshape(count, heads, HD), preferred_element_type=F32
        )
        * scale
    )
    scores = jnp.where(visible[:, None, :], scores, -1e30)
    newest = jnp.max(scores, axis=2)
    probs = jnp.where(visible[:, None, :], jnp.exp(scores - newest[:, :, None]), 0.0)
    total = jnp.sum(probs, axis=2)
    summed = jnp.einsum(
        "qhk,khd->qhd",
        probs.astype(BF16),
        values.reshape(count, heads, HD),
        preferred_element_type=F32,
    )
    return (summed / total[:, :, None]).reshape(rows, heads * HD).astype(BF16)

SHARED = 2560
OVER_X = 1792
FIRST = [1, 3, 0]
LAST = [2]

VMEM = pl.BlockSpec(memory_space=pltpu.VMEM)
SMEM = pl.BlockSpec(memory_space=pltpu.SMEM)
MIB = 1024 * 1024
LANES = 128


def call(body, out_shape, flops, moved, room, **kw):
    return pl.pallas_call(
        body,
        out_shape=out_shape,
        compiler_params=pltpu.CompilerParams(vmem_limit_bytes=room * MIB),
        cost_estimate=pl.CostEstimate(flops=flops, bytes_accessed=moved, transcendentals=0),
        **kw,
    )


def prepare(tokens, expert_ids, route_weight, at_x, experts):
    rows, width = tokens.shape
    split = (width - SHARED) // 2

    def body(x_ref, tokens, ids, weights, out, theirs):
        own = pl.ds(pl.multiple_of(SHARED + x_ref[0] * split, LANES), split)
        other = pl.ds(pl.multiple_of(SHARED + (1 - x_ref[0]) * split, LANES), split)
        out[:, :SHARED] = tokens[:, :SHARED]
        out[:, SHARED : SHARED + split] = tokens[:, own]
        theirs[...] = tokens[:, other]
        column = lax.broadcasted_iota(jnp.int32, (LANES, rows), 0)
        expert, term = column % experts, column // experts
        meta = jnp.zeros((LANES, rows), F32)
        for k in range(TOP):
            weight = jnp.broadcast_to(weights[k : k + 1, :], (LANES, rows))
            high = weight.astype(BF16).astype(F32)
            middle = (weight - high).astype(BF16).astype(F32)
            low = weight - high - middle
            value = jnp.where(term == 1, high, jnp.where(term == 2, middle, low))
            value = jnp.where(term == 0, 1.0, value)
            meta = jnp.where((ids[k : k + 1, :] == expert) & (term < 4), value, meta)
        eye = lax.broadcasted_iota(jnp.int32, (LANES, LANES), 0) == lax.broadcasted_iota(
            jnp.int32, (LANES, LANES), 1
        )
        meta = lax.dot_general(
            meta.astype(BF16),
            jnp.where(eye, 1.0, 0.0).astype(BF16),
            (((0,), (0,)), ((), ())),
            preferred_element_type=F32,
        )
        out[:, SHARED + split :] = meta.astype(BF16)

    return call(
        body,
        (
            jax.ShapeDtypeStruct((rows, SHARED + split + LANES), BF16),
            jax.ShapeDtypeStruct((rows, split), BF16),
        ),
        0,
        4 * rows * width,
        8,
        in_specs=[SMEM] + [VMEM] * 3,
        out_specs=(VMEM,) * 2,
    )(at_x.reshape(1), tokens, expert_ids.T, route_weight.T)


def pick(blocks, more, me, at_x, cap):
    count = len(blocks)
    rows, width = blocks[0].shape
    split = more[0].shape[1]
    edge = width - LANES
    features = edge + split
    step = count
    total = count + len(more)

    def body(s_ref, *refs):
        sources, (near, meta, other, placing, wide, *held, done) = refs[:total], refs[total:]
        copies = [
            pltpu.make_async_copy(source, to, done.at[i])
            for i, (source, to) in enumerate(zip(sources, held))
        ]
        for copy in copies:
            copy.start()
        for copy in copies:
            copy.wait()
        ins, extra = held[:count], held[count:]
        mine, x = s_ref[0], s_ref[1]
        lane = lax.broadcasted_iota(jnp.int32, (rows, LANES), 1)
        earlier = lax.broadcasted_iota(jnp.int32, (rows, rows), 0) > lax.broadcasted_iota(
            jnp.int32, (rows, rows), 1
        )
        slot = lax.broadcasted_iota(jnp.int32, (rows, cap), 1).astype(F32)
        own = pl.ds(pl.multiple_of(SHARED + x * split, LANES), split)
        theirs = pl.ds(pl.multiple_of(SHARED + (1 - x) * split, LANES), split)
        pieces = [
            ref[b * rows : (b + 1) * rows, :] for ref in extra for b in range(ref.shape[0] // rows)
        ]
        for begin in range(0, count, step):
            wide[...] = jnp.zeros_like(wide)
            for i in range(begin, begin + step):
                member = ins[i][:, edge:]
                rank = jnp.dot(earlier.astype(BF16), member, preferred_element_type=F32)
                member = member.astype(F32)
                local = i - begin
                for j in range(2):
                    at = lane == (mine if j == 0 else mine + 1 - 2 * (mine % 2))
                    hit = jnp.sum(jnp.where(at, member, 0.0), axis=1, keepdims=True)
                    place = jnp.sum(jnp.where(at, rank, 0.0), axis=1, keepdims=True)
                    onehot = jnp.where((place == slot) & (hit > 0.5), 1.0, 0.0).astype(BF16)
                    placing[i, :, j * cap : (j + 1) * cap] = onehot
                    column = (j * step + local) * cap
                    wide[local * rows : (local + 1) * rows, column : column + cap] = onehot
            onehot = wide[...]
            to = slice(begin * cap, (begin + step) * cap)

            def rows_of(parts):
                got = lax.dot_general(
                    onehot,
                    jnp.concatenate(parts, axis=0),
                    (((0,), (0,)), ((), ())),
                    preferred_element_type=F32,
                ).astype(BF16)
                return got[: step * cap], got[step * cap :]

            these = ins[begin : begin + step]
            near[to, :SHARED], other[to, :SHARED] = rows_of([r[:, :SHARED] for r in these])
            near[to, own], other[to, own] = rows_of([r[:, SHARED:edge] for r in these])
            near[to, theirs], other[to, theirs] = rows_of(pieces[begin : begin + step])
            meta[to, :], other[to, features:] = rows_of([r[:, edge:] for r in these])

    shape = lambda *s: jax.ShapeDtypeStruct(s, BF16)
    return call(
        body,
        (
            shape(count * cap, features),
            shape(count * cap, LANES),
            shape(count * cap, features + LANES),
            shape(count, rows, 2 * cap),
        ),
        4 * count * cap * rows * features,
        2 * count * (rows + 2 * cap) * features,
        20,
        in_specs=[SMEM] + [pl.BlockSpec(memory_space=pltpu.HBM)] * total,
        out_specs=(VMEM,) * 4,
        scratch_shapes=[pltpu.VMEM((step * rows, 2 * step * cap), BF16)]
        + [pltpu.VMEM(a.shape, BF16) for a in (*blocks, *more)]
        + [pltpu.SemaphoreType.DMA((total,))],
    )(jnp.stack([me, at_x]), *blocks, *more)


def mix(placing, near, far, far_first, first, count, at_x, late, adds=(), dtype=BF16):
    _, rows, both = placing.shape
    cap = both // 2
    half = near.shape[1] // 2
    rest = half - OVER_X
    width = OVER_X if late else half + rest

    def body(x_ref, placing, near, far, *refs):
        out = refs[-1]
        own = pl.multiple_of(x_ref[0] * half, LANES)
        other = pl.multiple_of((1 - x_ref[0]) * half, LANES)
        if late:
            parts = [(other, OVER_X, 0)]
        else:
            parts = [
                (own, OVER_X, 0),
                (pl.multiple_of(own + OVER_X, LANES), rest, OVER_X),
                (pl.multiple_of(other + OVER_X, LANES), rest, half),
            ]
        for start, size, to in parts:
            columns = pl.ds(start, size)
            slots = jnp.concatenate([near[:, columns], far[:, columns]], axis=0)
            total = jnp.dot(placing[0], slots, preferred_element_type=F32)
            for ref in refs[:-1]:
                if to + size <= ref.shape[1]:
                    total = total + ref[:, to : to + size].astype(F32)
            out[:, to : to + size] = total.astype(dtype)

    def at(base):
        return lambda g: (g + base, 0)

    return call(
        body,
        jax.ShapeDtypeStruct((count * rows, width), dtype),
        4 * count * rows * cap * width,
        2 * count * (rows + 2 * cap) * width,
        12,
        grid=(count,),
        in_specs=[
            SMEM,
            pl.BlockSpec((1, rows, both), lambda g: (g + first, 0, 0)),
            pl.BlockSpec((cap, 2 * half), at(first)),
            pl.BlockSpec((cap, 2 * half), at(first - far_first)),
        ]
        + [pl.BlockSpec((rows, a.shape[1]), at(base)) for a, base in adds],
        out_specs=pl.BlockSpec((rows, width), at(0)),
    )(at_x.reshape(1), placing, near, far, *[a for a, _ in adds])


def attend_pair(q_input, k_input, v_input, docs, past, at_x):
    rows, width = q_input.shape
    scale = HD ** (-0.5)
    turn = (((1,), (1,)), ((), ()))

    def body(x_ref, q, k, v, docs, past_k, past_v, past_docs, out, bias):
        @pl.when(pl.program_id(0) == 0)
        def _():
            i = lax.broadcasted_iota(jnp.int32, (rows, rows), 0)
            j = lax.broadcasted_iota(jnp.int32, (rows, rows), 1)
            same = lax.dot_general(docs[...], past_docs[...], turn, preferred_element_type=F32)
            bias[:, :rows] = jnp.where((same > 0.5) & (x_ref[0] > 0), 0.0, -1e30)
            same = lax.dot_general(docs[...], docs[...], turn, preferred_element_type=F32)
            bias[:, rows:] = jnp.where((same > 0.5) & (j <= i), 0.0, -1e30)

        query = q[...]
        early = lax.dot_general(query, past_k[...], turn, preferred_element_type=F32)
        late = lax.dot_general(query, k[...], turn, preferred_element_type=F32)
        early = early * scale + bias[:, :rows]
        late = late * scale + bias[:, rows:]
        top = jnp.maximum(
            jnp.max(early, axis=1, keepdims=True), jnp.max(late, axis=1, keepdims=True)
        )
        early, late = jnp.exp(early - top), jnp.exp(late - top)
        total = jnp.sum(early, axis=1, keepdims=True) + jnp.sum(late, axis=1, keepdims=True)
        mixed = jnp.dot(early.astype(BF16), past_v[...], preferred_element_type=F32) + jnp.dot(
            late.astype(BF16), v[...], preferred_element_type=F32
        )
        out[...] = (mixed / total).astype(BF16)

    heads = width // HD
    head = pl.BlockSpec((rows, HD), lambda h: (0, h))
    return call(
        body,
        jax.ShapeDtypeStruct((rows, width), BF16),
        8 * rows * rows * width,
        14 * rows * width,
        14,
        grid=(heads,),
        in_specs=[
            SMEM,
            head,
            head,
            head,
            pl.BlockSpec((rows, LANES), lambda h: (0, 0)),
            head,
            pl.BlockSpec((rows, HD), lambda h: (0, heads + h)),
            pl.BlockSpec((rows, LANES), lambda h: (0, 2 * heads)),
        ],
        out_specs=head,
        scratch_shapes=[pltpu.VMEM((rows, 2 * rows), F32)],
    )(at_x.reshape(1), q_input, k_input, v_input, docs, past, past, past)


def spread(onehot):
    blocks, cap, rows = onehot.shape
    same = jnp.eye(blocks, dtype=jnp.bool_)
    wide = onehot[:, :, None, :] & same[:, None, :, None]
    return wide.reshape(blocks * cap, blocks * rows).astype(BF16)


def solution(mesh):
    n_ctx = mesh.shape["ctx"]
    n_exp = mesh.shape["exp"]
    nz = n_exp // 4

    def pairs(move):
        out = []
        for i in range(n_exp):
            z, y, c = i // 4, (i // 2) % 2, i % 2
            z, y, c = move(z, y, c)
            out.append((i, (z % nz * 2 + y) * 2 + c))
        return out

    def z_shift(x, d):
        return lax.ppermute(x, "exp", pairs(lambda z, y, c: (z + d, y, c)))

    def y_swap(x):
        return lax.ppermute(x, "exp", pairs(lambda z, y, c: (z, 1 - y, c)))

    def core_swap(x):
        return lax.ppermute(x, "exp", pairs(lambda z, y, c: (z, y, 1 - c)))

    def x_swap(x):
        return lax.ppermute(x, "ctx", [(0, 1), (1, 0)])

    def on_device(
        q_input, k_input, v_input, segment_ids, tokens, expert_ids, route_weight, w_in, w_down
    ):
        me = lax.axis_index("exp")
        at_x = lax.axis_index("ctx")
        rows, width = tokens.shape
        cap = rows * 8 // n_exp
        half = width // 2
        near = n_exp // 2
        slots = near * cap

        if n_ctx == 2:
            plan = [("x", 1024), ("x", 1024), ("", 1024), ("x", 1024), ("", 1024)]
        else:
            plan = [("", width)]
        arrived = []
        start = 0
        for kind, size in plan:
            if kind == "x":
                block = lax.dynamic_slice_in_dim(tokens, start + at_x * (size // 2), size // 2, 1)
            else:
                block = tokens[:, start : start + size]
            line = jnp.concatenate([block] + [z_shift(block, d) for d in range(1, nz)], axis=0)
            both = jnp.concatenate([line, y_swap(line)], axis=0)
            if kind == "x":
                other = x_swap(both)
                both = jnp.concatenate(
                    [jnp.where(at_x == 0, both, other), jnp.where(at_x == 0, other, both)], axis=1
                )
            arrived.append((start, size, both))
            start += size

        meta = jnp.concatenate([expert_ids.astype(F32), route_weight], axis=1)
        meta = lax.all_gather(meta, "exp", axis=0, tiled=False)
        z, y, c = me // 4, (me // 2) % 2, me % 2
        order = jnp.stack(
            [
                ((z - d + nz) % nz * 2 + (y + yr) % 2) * 2 + (c + cr) % 2
                for cr in range(2)
                for yr in range(2)
                for d in range(nz)
            ]
        )
        meta = meta[order]
        ids, weights = meta[:, :, :TOP].astype(jnp.int32), meta[:, :, TOP:]

        def placing(ids, expert):
            named = ids == expert
            hit = jnp.any(named, axis=2)
            count = hit.astype(jnp.int32)
            rank = jnp.cumsum(count, axis=1) - count
            slot = jnp.arange(cap, dtype=jnp.int32)
            return named, hit[:, None, :] & (rank[:, None, :] == slot[None, :, None])

        named, mine = placing(ids, me)
        _, others = placing(ids[:near], me + 1 - 2 * c)
        weight = jnp.sum(jnp.where(named, weights, 0.0), axis=2)
        weight = jnp.sum(jnp.where(mine, weight[:, None, :], 0.0), axis=2).reshape(2 * slots, 1)
        place = jnp.concatenate([spread(mine[:near]), spread(others)], axis=0)

        gate = up = None
        for start, size, both in arrived:
            placed = jnp.dot(place, both, preferred_element_type=F32).astype(BF16)
            block = jnp.concatenate([placed[:slots], core_swap(placed[slots:])], axis=0)
            g = jnp.dot(block, w_in[0, 0, start : start + size], preferred_element_type=F32)
            u = jnp.dot(block, w_in[0, 1, start : start + size], preferred_element_type=F32)
            gate = g if gate is None else gate + g
            up = u if up is None else up + u
        hidden = (jax.nn.silu(gate) * up).astype(BF16)

        if n_ctx == 2:
            back = [("x", 512), ("x", 512), ("", 512), ("x", 512), ("", 512)]
        else:
            back = [("", half)]
        down = w_down[0]
        pieces = []
        start = 0
        for kind, size in back:
            if n_ctx == 2:
                cols = jnp.concatenate(
                    [down[:, start : start + size], down[:, half + start : half + start + size]],
                    axis=1,
                )
            else:
                cols = down
            part = jnp.dot(hidden, cols, preferred_element_type=F32)
            part = (part * weight).astype(BF16)
            part = jnp.concatenate([part[:slots], core_swap(part[slots:])], axis=0)
            summed = lax.dot_general(
                place, part, (((0,), (0,)), ((), ())), preferred_element_type=F32
            )

            def over_x(summed):
                first, second = summed[:, :size].astype(BF16), summed[:, size:].astype(BF16)
                other = x_swap(jnp.where(at_x == 0, second, first))
                own = jnp.where(at_x == 0, summed[:, :size], summed[:, size:])
                return own + other.astype(F32)

            if kind == "x":
                summed = over_x(summed)
            count = nz * rows
            summed = summed[:count] + y_swap(summed[count:].astype(BF16)).astype(F32)
            total = summed[:rows]
            for d in range(1, nz):
                block = summed[d * rows : (d + 1) * rows].astype(BF16)
                total = total + z_shift(block, -d).astype(F32)
            if kind != "x":
                if n_ctx == 2:
                    total = over_x(total)
                else:
                    total = lax.psum_scatter(
                        total.astype(BF16), "ctx", scatter_dimension=1, tiled=True
                    )
            pieces.append(total.astype(BF16))
            start += size
        moe_out = jnp.concatenate(pieces, axis=1)
        attn_out = attend(q_input, k_input, v_input, segment_ids, n_ctx)
        return attn_out, moe_out

    def pair_device(
        q_input, k_input, v_input, segment_ids, tokens, expert_ids, route_weight, w_in, w_down
    ):
        me = lax.axis_index("exp")
        at_x = lax.axis_index("ctx")
        rows, width = tokens.shape
        cap = rows * 8 // n_exp
        half = width // 2
        split = (width - SHARED) // 2
        after = lax.optimization_barrier

        block, theirs = prepare(tokens, expert_ids, route_weight, at_x, n_exp)
        cut = lambda a: a[:, SHARED : SHARED + split]
        both = lambda d: jnp.concatenate([cut(line[d]), cut(across[d])], axis=0)
        line = {0: block, 1: z_shift(block, 1)}
        across = {0: y_swap(block)}
        line[1], again = after((line[1], block))
        line[3] = z_shift(again, -1)
        line[3], again = after((line[3], line[1]))
        line[2] = z_shift(again, 1)
        block, segment_ids, k_input = after((block, segment_ids, k_input))
        docs = segment_ids[:, None] == jnp.arange(LANES, dtype=jnp.int32)
        docs = docs.astype(BF16)
        past = lax.ppermute(jnp.concatenate([k_input, v_input, docs], axis=1), "ctx", [(0, 1)])
        line[1], across[0] = after((line[1], across[0]))
        across[1] = y_swap(line[1])
        line[3], across[1] = after((line[3], across[1]))
        across[3] = y_swap(line[3])
        across[0], past = after((across[0], past))
        more = {0: [theirs, x_swap(cut(across[0]))], 1: [x_swap(both(1))]}
        line[2], across[3], before = after((line[2], across[3], more[0][1]))
        more[0][1] = before
        across[2] = y_swap(line[2])
        more[3] = [x_swap(both(3))]
        line[2], before = after((line[2], more[1][0]))
        more[1] = [before]
        more[2] = [x_swap(cut(line[2]))]
        attn_out = attend_pair(q_input, k_input, v_input, docs, past, at_x)
        across[2], before, attn_out = after((across[2], more[3][0], attn_out))
        more[3] = [before]
        more[2].append(x_swap(cut(across[2])))

        def place(group, extra):
            return pick(
                [b for d in group for b in (line[d], across[d])], extra, me, at_x, cap
            )

        early, early_meta, early_sent, early_placing = place(
            FIRST, [a for d in FIRST for a in more[d]]
        )
        early_far = core_swap(early_sent)
        more[2][1], early = after((more[2][1], early))
        near, meta, sent, placing = place(LAST, more[2])
        far = core_swap(sent)
        join = lambda *parts: jnp.concatenate(parts, axis=0)
        placing = join(placing, early_placing)
        near, meta = join(near, early), join(meta, early_meta)
        far = join(far, early_far)

        def expert(block, meta):
            gate = jnp.dot(block, w_in[0, 0], preferred_element_type=F32)
            up = jnp.dot(block, w_in[0, 1], preferred_element_type=F32)
            gate, up = after((gate, up))
            hidden = (jax.nn.silu(gate) * up).astype(BF16)
            lane = jnp.arange(LANES, dtype=jnp.int32)
            at = (lane % n_exp == me) & (lane >= n_exp) & (lane < 4 * n_exp)
            scale = jnp.sum(jnp.where(at, meta.astype(F32), 0.0), axis=1, keepdims=True)
            hidden, scale = after((hidden, scale))
            out = jnp.dot(hidden, w_down[0], preferred_element_type=F32)
            return (out * scale).astype(BF16)

        near = expert(near, meta)
        near, far = after((near, far))
        sent = expert(far[:, :width], far[:, width:])
        edge = sent.shape[0] // 2
        far_a = core_swap(sent[:edge])
        far_a, rest = after((far_a, sent[edge:]))
        far_b = core_swap(rest)

        def sums(i, count, late, adds=(), dtype=BF16):
            far, begin = (far_a, 0) if i < 4 else (far_b, 4)
            return mix(placing, near, far, begin, i, count, at_x, late, adds, dtype)

        got_x = []
        for i in range(4):
            late = sums(2 * i, 2, True)
            near, late = after((near, late))
            got_x.append(x_swap(late))

        def over_y(i):
            return y_swap(sums(2 * i + 1, 1, False, [(got_x[i], 1)]))

        got_y = [over_y(0)]
        turn = sums(3, 1, False, [(got_x[1], 1)])
        got_y[0], turn = after((got_y[0], turn))
        got_y.append(y_swap(turn))
        part = sums(0, 1, False, [(got_x[0], 0), (got_y[0], 0)])
        part = z_shift(part, -1)
        got_x[2], part = after((got_x[2], part))
        got_y.append(over_y(2))
        part = sums(2, 1, False, [(got_x[1], 0), (got_y[1], 0), (part, 0)])
        right = z_shift(part, -1)
        got_x[3], right = after((got_x[3], right))
        got_y.append(over_y(3))
        left = z_shift(sums(4, 1, False, [(got_x[2], 0), (got_y[2], 0)]), 1)
        total = sums(6, 1, False, [(got_x[3], 0), (got_y[3], 0)], F32)
        total = total + right.astype(F32) + left.astype(F32)
        got = x_swap(total[:, half:].astype(BF16))
        moe_out = jnp.concatenate(
            [total[:, :OVER_X], total[:, OVER_X:half] + got.astype(F32)], axis=1
        ).astype(BF16)
        return attn_out, moe_out

    in_specs = (
        P("ctx", "exp"),
        P("ctx", "exp"),
        P("ctx", "exp"),
        P("ctx"),
        P("exp", None),
        P("exp", None),
        P("exp", None),
        P("exp", None, None, "ctx"),
        P("exp", "ctx", None),
    )
    out_specs = (P("ctx", "exp"), P("exp", "ctx"))
    return jax.shard_map(
        pair_device if n_ctx == 2 and nz == 4 else on_device,
        mesh=mesh,
        in_specs=in_specs,
        out_specs=out_specs,
        check_vma=False,
    )
```

```python
import jax
import jax.numpy as jnp
from jax import lax
from jax.experimental import pallas as pl
from jax.experimental.pallas import tpu as pltpu
from jax.sharding import PartitionSpec as P

HD = 128
TOP = 6
BF16 = jnp.bfloat16
F32 = jnp.float32


def attend(q_input, k_input, v_input, segment_ids, n_ctx):
    scale = HD ** (-0.5)
    rows = q_input.shape[0]
    heads = q_input.shape[1] // HD
    place = lax.axis_index("ctx") * rows + jnp.arange(rows, dtype=jnp.int32)
    if n_ctx == 2:
        ahead = [(0, 1)]
        keys = jnp.concatenate([lax.ppermute(k_input, "ctx", ahead), k_input], axis=0)
        values = jnp.concatenate([lax.ppermute(v_input, "ctx", ahead), v_input], axis=0)
        docs = jnp.concatenate([lax.ppermute(segment_ids, "ctx", ahead), segment_ids], axis=0)
        first = (lax.axis_index("ctx") - 1) * rows
    else:
        keys = lax.all_gather(k_input, "ctx", axis=0, tiled=True)
        values = lax.all_gather(v_input, "ctx", axis=0, tiled=True)
        docs = lax.all_gather(segment_ids, "ctx", axis=0, tiled=True)
        first = 0
    count = keys.shape[0]
    key_place = first + jnp.arange(count, dtype=jnp.int32)
    visible = (
        (key_place[None, :] <= place[:, None])
        & (key_place[None, :] >= 0)
        & (docs[None, :] == segment_ids[:, None])
    )
    queries = q_input.reshape(rows, heads, HD)
    scores = (
        jnp.einsum(
            "qhd,khd->qhk", queries, keys.reshape(count, heads, HD), preferred_element_type=F32
        )
        * scale
    )
    scores = jnp.where(visible[:, None, :], scores, -1e30)
    newest = jnp.max(scores, axis=2)
    probs = jnp.where(visible[:, None, :], jnp.exp(scores - newest[:, :, None]), 0.0)
    total = jnp.sum(probs, axis=2)
    summed = jnp.einsum(
        "qhk,khd->qhd",
        probs.astype(BF16),
        values.reshape(count, heads, HD),
        preferred_element_type=F32,
    )
    return (summed / total[:, :, None]).reshape(rows, heads * HD).astype(BF16)

SHARED = 2560
OVER_X = 1792
FIRST = [1, 3, 0]
LAST = [2]

VMEM = pl.BlockSpec(memory_space=pltpu.VMEM)
SMEM = pl.BlockSpec(memory_space=pltpu.SMEM)
MIB = 1024 * 1024
LANES = 128
SUBLANES = 16


def call(body, out_shape, flops, moved, room, **kw):
    return pl.pallas_call(
        body,
        out_shape=out_shape,
        compiler_params=pltpu.CompilerParams(vmem_limit_bytes=room * MIB),
        cost_estimate=pl.CostEstimate(flops=flops, bytes_accessed=moved, transcendentals=0),
        **kw,
    )


def prepare(tokens, expert_ids, route_weight, at_x, experts):
    rows, width = tokens.shape
    split = (width - SHARED) // 2

    def body(x_ref, tokens, ids, weights, out, theirs):
        own = pl.ds(pl.multiple_of(SHARED + x_ref[0] * split, LANES), split)
        other = pl.ds(pl.multiple_of(SHARED + (1 - x_ref[0]) * split, LANES), split)
        out[:, :SHARED] = tokens[:, :SHARED]
        out[:, SHARED : SHARED + split] = tokens[:, own]
        theirs[...] = tokens[:, other]
        column = lax.broadcasted_iota(jnp.int32, (LANES, rows), 0)
        expert, term = column % experts, column // experts
        meta = jnp.zeros((LANES, rows), F32)
        for k in range(TOP):
            weight = jnp.broadcast_to(weights[k : k + 1, :], (LANES, rows))
            high = weight.astype(BF16).astype(F32)
            middle = (weight - high).astype(BF16).astype(F32)
            low = weight - high - middle
            value = jnp.where(term == 1, high, jnp.where(term == 2, middle, low))
            value = jnp.where(term == 0, 1.0, value)
            meta = jnp.where((ids[k : k + 1, :] == expert) & (term < 4), value, meta)
        eye = lax.broadcasted_iota(jnp.int32, (LANES, LANES), 0) == lax.broadcasted_iota(
            jnp.int32, (LANES, LANES), 1
        )
        meta = lax.dot_general(
            meta.astype(BF16),
            jnp.where(eye, 1.0, 0.0).astype(BF16),
            (((0,), (0,)), ((), ())),
            preferred_element_type=F32,
        )
        out[:, SHARED + split :] = meta.astype(BF16)

    return call(
        body,
        (
            jax.ShapeDtypeStruct((rows, SHARED + split + LANES), BF16),
            jax.ShapeDtypeStruct((rows, split), BF16),
        ),
        0,
        4 * rows * width,
        8,
        in_specs=[SMEM] + [VMEM] * 3,
        out_specs=(VMEM,) * 2,
    )(at_x.reshape(1), tokens, expert_ids.T, route_weight.T)


def pick(blocks, more, me, at_x, cap):
    count = len(blocks)
    rows, width = blocks[0].shape
    split = more[0].shape[1]
    edge = width - LANES
    features = edge + split
    step = count
    total = count + len(more)

    def body(s_ref, *refs):
        sources, (near, meta, other, placing, wide, *held, done) = refs[:total], refs[total:]
        copies = [
            pltpu.make_async_copy(source, to, done.at[i])
            for i, (source, to) in enumerate(zip(sources, held))
        ]
        for copy in copies:
            copy.start()
        for copy in copies:
            copy.wait()
        ins, extra = held[:count], held[count:]
        mine, x = s_ref[0], s_ref[1]
        lane = lax.broadcasted_iota(jnp.int32, (rows, LANES), 1)
        earlier = lax.broadcasted_iota(jnp.int32, (rows, rows), 0) > lax.broadcasted_iota(
            jnp.int32, (rows, rows), 1
        )
        slot = lax.broadcasted_iota(jnp.int32, (rows, cap), 1).astype(F32)
        own = pl.ds(pl.multiple_of(SHARED + x * split, LANES), split)
        theirs = pl.ds(pl.multiple_of(SHARED + (1 - x) * split, LANES), split)
        pieces = [
            ref[b * rows : (b + 1) * rows, :] for ref in extra for b in range(ref.shape[0] // rows)
        ]
        for begin in range(0, count, step):
            wide[...] = jnp.zeros_like(wide)
            for i in range(begin, begin + step):
                member = ins[i][:, edge:]
                rank = jnp.dot(earlier.astype(BF16), member, preferred_element_type=F32)
                member = member.astype(F32)
                local = i - begin
                for j in range(2):
                    at = lane == (mine if j == 0 else mine + 1 - 2 * (mine % 2))
                    hit = jnp.sum(jnp.where(at, member, 0.0), axis=1, keepdims=True)
                    place = jnp.sum(jnp.where(at, rank, 0.0), axis=1, keepdims=True)
                    onehot = jnp.where((place == slot) & (hit > 0.5), 1.0, 0.0).astype(BF16)
                    placing[i, :, j * cap : (j + 1) * cap] = onehot
                    column = (j * step + local) * cap
                    wide[local * rows : (local + 1) * rows, column : column + cap] = onehot
            onehot = wide[...]
            to = slice(begin * cap, (begin + step) * cap)

            def rows_of(parts):
                got = lax.dot_general(
                    onehot,
                    jnp.concatenate(parts, axis=0),
                    (((0,), (0,)), ((), ())),
                    preferred_element_type=F32,
                ).astype(BF16)
                return got[: step * cap], got[step * cap :]

            these = ins[begin : begin + step]
            near[to, :SHARED], other[to, :SHARED] = rows_of([r[:, :SHARED] for r in these])
            near[to, own], other[to, own] = rows_of([r[:, SHARED:edge] for r in these])
            near[to, theirs], other[to, theirs] = rows_of(pieces[begin : begin + step])
            meta[to, :], other[to, features:] = rows_of([r[:, edge:] for r in these])

    shape = lambda *s: jax.ShapeDtypeStruct(s, BF16)
    return call(
        body,
        (
            shape(count * cap, features),
            shape(count * cap, LANES),
            shape(count * cap, features + LANES),
            shape(count, rows, 2 * cap),
        ),
        40 * count * cap * rows * features,
        2 * count * (rows + 2 * cap) * features,
        20,
        in_specs=[SMEM] + [pl.BlockSpec(memory_space=pltpu.HBM)] * total,
        out_specs=(VMEM,) * 4,
        scratch_shapes=[pltpu.VMEM((step * rows, 2 * step * cap), BF16)]
        + [pltpu.VMEM(a.shape, BF16) for a in (*blocks, *more)]
        + [pltpu.SemaphoreType.DMA((total,))],
    )(jnp.stack([me, at_x]), *blocks, *more)


def mix(placing, near, far, far_first, first, count, at_x, late, adds=(), dtype=BF16):
    _, rows, both = placing.shape
    cap = both // 2
    half = near.shape[1] // 2
    rest = half - OVER_X
    width = OVER_X if late else half + rest

    def body(x_ref, placing, near, far, *refs):
        out = refs[-1]
        own = pl.multiple_of(x_ref[0] * half, LANES)
        other = pl.multiple_of((1 - x_ref[0]) * half, LANES)
        if late:
            parts = [(other, OVER_X, 0)]
        else:
            parts = [
                (own, OVER_X, 0),
                (pl.multiple_of(own + OVER_X, LANES), rest, OVER_X),
                (pl.multiple_of(other + OVER_X, LANES), rest, half),
            ]
        for start, size, to in parts:
            columns = pl.ds(start, size)
            slots = jnp.concatenate([near[:, columns], far[:, columns]], axis=0)
            total = jnp.dot(placing[0], slots, preferred_element_type=F32)
            for ref in refs[:-1]:
                if to + size <= ref.shape[1]:
                    total = total + ref[:, to : to + size].astype(F32)
            out[:, to : to + size] = total.astype(dtype)

    def at(base):
        return lambda g: (g + base, 0)

    return call(
        body,
        jax.ShapeDtypeStruct((count * rows, width), dtype),
        4 * count * rows * cap * width,
        2 * count * (rows + 2 * cap) * width,
        12,
        grid=(count,),
        in_specs=[
            SMEM,
            pl.BlockSpec((1, rows, both), lambda g: (g + first, 0, 0)),
            pl.BlockSpec((cap, 2 * half), at(first)),
            pl.BlockSpec((cap, 2 * half), at(first - far_first)),
        ]
        + [pl.BlockSpec((rows, a.shape[1]), at(base)) for a, base in adds],
        out_specs=pl.BlockSpec((rows, width), at(0)),
    )(at_x.reshape(1), placing, near, far, *[a for a, _ in adds])


def attend_pair(q_input, k_input, v_input, segment_ids, past, at_x):
    rows, width = q_input.shape
    scale = HD ** (-0.5)
    turn = (((1,), (1,)), ((), ()))

    def body(x_ref, q, k, v, down, along, past_k, past_v, past_docs, out, bias):
        @pl.when(pl.program_id(0) == 0)
        def _():
            i = lax.broadcasted_iota(jnp.int32, (rows, rows), 0)
            j = lax.broadcasted_iota(jnp.int32, (rows, rows), 1)
            same = down[...] == past_docs[:1, :].astype(F32)
            bias[:, :rows] = jnp.where(same & (x_ref[0] > 0), 0.0, -1e30)
            bias[:, rows:] = jnp.where((down[...] == along[...]) & (j <= i), 0.0, -1e30)

        query = q[...]
        early = lax.dot_general(query, past_k[...], turn, preferred_element_type=F32)
        late = lax.dot_general(query, k[...], turn, preferred_element_type=F32)
        early = early * scale + bias[:, :rows]
        late = late * scale + bias[:, rows:]
        top = jnp.maximum(
            jnp.max(early, axis=1, keepdims=True), jnp.max(late, axis=1, keepdims=True)
        )
        early, late = jnp.exp(early - top), jnp.exp(late - top)
        total = jnp.sum(early, axis=1, keepdims=True) + jnp.sum(late, axis=1, keepdims=True)
        mixed = jnp.dot(early.astype(BF16), past_v[...], preferred_element_type=F32) + jnp.dot(
            late.astype(BF16), v[...], preferred_element_type=F32
        )
        out[...] = (mixed / total).astype(BF16)

    heads = width // HD
    head = pl.BlockSpec((rows, HD), lambda h: (0, h))
    return call(
        body,
        jax.ShapeDtypeStruct((rows, width), BF16),
        48 * rows * rows * width,
        14 * rows * width,
        14,
        grid=(heads,),
        in_specs=[
            SMEM,
            head,
            head,
            head,
            pl.BlockSpec((rows, 1), lambda h: (0, 0)),
            pl.BlockSpec((1, rows), lambda h: (0, 0)),
            head,
            pl.BlockSpec((rows, HD), lambda h: (1, h)),
            pl.BlockSpec((SUBLANES, rows), lambda h: (2 * rows // SUBLANES, 0)),
        ],
        out_specs=head,
        scratch_shapes=[pltpu.VMEM((rows, 2 * rows), F32)],
    )(
        at_x.reshape(1),
        q_input,
        k_input,
        v_input,
        segment_ids.astype(F32)[:, None],
        segment_ids.astype(F32)[None, :],
        past,
        past,
        past,
    )


def spread(onehot):
    blocks, cap, rows = onehot.shape
    same = jnp.eye(blocks, dtype=jnp.bool_)
    wide = onehot[:, :, None, :] & same[:, None, :, None]
    return wide.reshape(blocks * cap, blocks * rows).astype(BF16)


def solution(mesh):
    n_ctx = mesh.shape["ctx"]
    n_exp = mesh.shape["exp"]
    nz = n_exp // 4

    def pairs(move):
        out = []
        for i in range(n_exp):
            z, y, c = i // 4, (i // 2) % 2, i % 2
            z, y, c = move(z, y, c)
            out.append((i, (z % nz * 2 + y) * 2 + c))
        return out

    def z_shift(x, d):
        return lax.ppermute(x, "exp", pairs(lambda z, y, c: (z + d, y, c)))

    def y_swap(x):
        return lax.ppermute(x, "exp", pairs(lambda z, y, c: (z, 1 - y, c)))

    def core_swap(x):
        return lax.ppermute(x, "exp", pairs(lambda z, y, c: (z, y, 1 - c)))

    def x_swap(x):
        return lax.ppermute(x, "ctx", [(0, 1), (1, 0)])

    def on_device(
        q_input, k_input, v_input, segment_ids, tokens, expert_ids, route_weight, w_in, w_down
    ):
        me = lax.axis_index("exp")
        at_x = lax.axis_index("ctx")
        rows, width = tokens.shape
        cap = rows * 8 // n_exp
        half = width // 2
        near = n_exp // 2
        slots = near * cap

        if n_ctx == 2:
            plan = [("x", 1024), ("x", 1024), ("", 1024), ("x", 1024), ("", 1024)]
        else:
            plan = [("", width)]
        arrived = []
        start = 0
        for kind, size in plan:
            if kind == "x":
                block = lax.dynamic_slice_in_dim(tokens, start + at_x * (size // 2), size // 2, 1)
            else:
                block = tokens[:, start : start + size]
            line = jnp.concatenate([block] + [z_shift(block, d) for d in range(1, nz)], axis=0)
            both = jnp.concatenate([line, y_swap(line)], axis=0)
            if kind == "x":
                other = x_swap(both)
                both = jnp.concatenate(
                    [jnp.where(at_x == 0, both, other), jnp.where(at_x == 0, other, both)], axis=1
                )
            arrived.append((start, size, both))
            start += size

        meta = jnp.concatenate([expert_ids.astype(F32), route_weight], axis=1)
        meta = lax.all_gather(meta, "exp", axis=0, tiled=False)
        z, y, c = me // 4, (me // 2) % 2, me % 2
        order = jnp.stack(
            [
                ((z - d + nz) % nz * 2 + (y + yr) % 2) * 2 + (c + cr) % 2
                for cr in range(2)
                for yr in range(2)
                for d in range(nz)
            ]
        )
        meta = meta[order]
        ids, weights = meta[:, :, :TOP].astype(jnp.int32), meta[:, :, TOP:]

        def placing(ids, expert):
            named = ids == expert
            hit = jnp.any(named, axis=2)
            count = hit.astype(jnp.int32)
            rank = jnp.cumsum(count, axis=1) - count
            slot = jnp.arange(cap, dtype=jnp.int32)
            return named, hit[:, None, :] & (rank[:, None, :] == slot[None, :, None])

        named, mine = placing(ids, me)
        _, others = placing(ids[:near], me + 1 - 2 * c)
        weight = jnp.sum(jnp.where(named, weights, 0.0), axis=2)
        weight = jnp.sum(jnp.where(mine, weight[:, None, :], 0.0), axis=2).reshape(2 * slots, 1)
        place = jnp.concatenate([spread(mine[:near]), spread(others)], axis=0)

        gate = up = None
        for start, size, both in arrived:
            placed = jnp.dot(place, both, preferred_element_type=F32).astype(BF16)
            block = jnp.concatenate([placed[:slots], core_swap(placed[slots:])], axis=0)
            g = jnp.dot(block, w_in[0, 0, start : start + size], preferred_element_type=F32)
            u = jnp.dot(block, w_in[0, 1, start : start + size], preferred_element_type=F32)
            gate = g if gate is None else gate + g
            up = u if up is None else up + u
        hidden = (jax.nn.silu(gate) * up).astype(BF16)

        if n_ctx == 2:
            back = [("x", 512), ("x", 512), ("", 512), ("x", 512), ("", 512)]
        else:
            back = [("", half)]
        down = w_down[0]
        pieces = []
        start = 0
        for kind, size in back:
            if n_ctx == 2:
                cols = jnp.concatenate(
                    [down[:, start : start + size], down[:, half + start : half + start + size]],
                    axis=1,
                )
            else:
                cols = down
            part = jnp.dot(hidden, cols, preferred_element_type=F32)
            part = (part * weight).astype(BF16)
            part = jnp.concatenate([part[:slots], core_swap(part[slots:])], axis=0)
            summed = lax.dot_general(
                place, part, (((0,), (0,)), ((), ())), preferred_element_type=F32
            )

            def over_x(summed):
                first, second = summed[:, :size].astype(BF16), summed[:, size:].astype(BF16)
                other = x_swap(jnp.where(at_x == 0, second, first))
                own = jnp.where(at_x == 0, summed[:, :size], summed[:, size:])
                return own + other.astype(F32)

            if kind == "x":
                summed = over_x(summed)
            count = nz * rows
            summed = summed[:count] + y_swap(summed[count:].astype(BF16)).astype(F32)
            total = summed[:rows]
            for d in range(1, nz):
                block = summed[d * rows : (d + 1) * rows].astype(BF16)
                total = total + z_shift(block, -d).astype(F32)
            if kind != "x":
                if n_ctx == 2:
                    total = over_x(total)
                else:
                    total = lax.psum_scatter(
                        total.astype(BF16), "ctx", scatter_dimension=1, tiled=True
                    )
            pieces.append(total.astype(BF16))
            start += size
        moe_out = jnp.concatenate(pieces, axis=1)
        attn_out = attend(q_input, k_input, v_input, segment_ids, n_ctx)
        return attn_out, moe_out

    def pair_device(
        q_input, k_input, v_input, segment_ids, tokens, expert_ids, route_weight, w_in, w_down
    ):
        if q_input.shape[0] != q_input.shape[1]:
            return on_device(
                q_input,
                k_input,
                v_input,
                segment_ids,
                tokens,
                expert_ids,
                route_weight,
                w_in,
                w_down,
            )
        me = lax.axis_index("exp")
        at_x = lax.axis_index("ctx")
        rows, width = tokens.shape
        cap = rows * 8 // n_exp
        half = width // 2
        split = (width - SHARED) // 2
        after = lax.optimization_barrier

        block, theirs = prepare(tokens, expert_ids, route_weight, at_x, n_exp)
        cut = lambda a: a[:, SHARED : SHARED + split]
        both = lambda d: jnp.concatenate([cut(line[d]), cut(across[d])], axis=0)
        line = {0: block, 1: z_shift(block, 1)}
        across = {0: y_swap(block)}
        line[1], again = after((line[1], block))
        line[3] = z_shift(again, -1)
        line[3], again = after((line[3], line[1]))
        line[2] = z_shift(again, 1)
        block, k_input = after((block, k_input))
        docs = jnp.broadcast_to(segment_ids.astype(BF16)[None, :], (SUBLANES, k_input.shape[1]))
        past = lax.ppermute(jnp.concatenate([k_input, v_input, docs], axis=0), "ctx", [(0, 1)])
        line[1], across[0] = after((line[1], across[0]))
        across[1] = y_swap(line[1])
        line[3], across[1] = after((line[3], across[1]))
        across[3] = y_swap(line[3])
        across[0], past = after((across[0], past))
        more = {0: [theirs, x_swap(cut(across[0]))], 1: [x_swap(both(1))]}
        line[2], across[3], before = after((line[2], across[3], more[0][1]))
        more[0][1] = before
        across[2] = y_swap(line[2])
        more[3] = [x_swap(both(3))]
        line[2], before = after((line[2], more[1][0]))
        more[1] = [before]
        more[2] = [x_swap(cut(line[2]))]
        attn_out = attend_pair(q_input, k_input, v_input, segment_ids, past, at_x)
        across[2], before, attn_out = after((across[2], more[3][0], attn_out))
        more[3] = [before]
        more[2].append(x_swap(cut(across[2])))

        def place(group, extra):
            return pick(
                [b for d in group for b in (line[d], across[d])], extra, me, at_x, cap
            )

        early, early_meta, early_sent, early_placing = place(
            FIRST, [a for d in FIRST for a in more[d]]
        )
        early_far = core_swap(early_sent)
        more[2][1], early = after((more[2][1], early))
        near, meta, sent, placing = place(LAST, more[2])
        far = core_swap(sent)
        join = lambda *parts: jnp.concatenate(parts, axis=0)
        placing = join(placing, early_placing)
        near, meta = join(near, early), join(meta, early_meta)
        far = join(far, early_far)

        def expert(block, meta):
            gate = jnp.dot(block, w_in[0, 0], preferred_element_type=F32)
            up = jnp.dot(block, w_in[0, 1], preferred_element_type=F32)
            gate, up = after((gate, up))
            hidden = (jax.nn.silu(gate) * up).astype(BF16)
            lane = jnp.arange(LANES, dtype=jnp.int32)
            at = (lane % n_exp == me) & (lane >= n_exp) & (lane < 4 * n_exp)
            scale = jnp.sum(jnp.where(at, meta.astype(F32), 0.0), axis=1, keepdims=True)
            hidden, scale = after((hidden, scale))
            out = jnp.dot(hidden, w_down[0], preferred_element_type=F32)
            return (out * scale).astype(BF16)

        near = expert(near, meta)
        near, far = after((near, far))
        sent = expert(far[:, :width], far[:, width:])
        edge = sent.shape[0] // 2
        far_a = core_swap(sent[:edge])
        far_a, rest = after((far_a, sent[edge:]))
        far_b = core_swap(rest)

        def sums(i, count, late, adds=(), dtype=BF16):
            far, begin = (far_a, 0) if i < 4 else (far_b, 4)
            return mix(placing, near, far, begin, i, count, at_x, late, adds, dtype)

        got_x = []
        for i in range(4):
            late = sums(2 * i, 2, True)
            near, late = after((near, late))
            got_x.append(x_swap(late))

        def over_y(i):
            return y_swap(sums(2 * i + 1, 1, False, [(got_x[i], 1)]))

        got_y = [over_y(0)]
        turn = sums(3, 1, False, [(got_x[1], 1)])
        got_y[0], turn = after((got_y[0], turn))
        got_y.append(y_swap(turn))
        part = sums(0, 1, False, [(got_x[0], 0), (got_y[0], 0)])
        part = z_shift(part, -1)
        got_x[2], part = after((got_x[2], part))
        got_y.append(over_y(2))
        part = sums(2, 1, False, [(got_x[1], 0), (got_y[1], 0), (part, 0)])
        right = z_shift(part, -1)
        got_x[3], right = after((got_x[3], right))
        got_y.append(over_y(3))
        left = z_shift(sums(4, 1, False, [(got_x[2], 0), (got_y[2], 0)]), 1)
        total = sums(6, 1, False, [(got_x[3], 0), (got_y[3], 0)], F32)
        total = total + right.astype(F32) + left.astype(F32)
        got = x_swap(total[:, half:].astype(BF16))
        moe_out = jnp.concatenate(
            [total[:, :OVER_X], total[:, OVER_X:half] + got.astype(F32)], axis=1
        ).astype(BF16)
        return attn_out, moe_out

    in_specs = (
        P("ctx", "exp"),
        P("ctx", "exp"),
        P("ctx", "exp"),
        P("ctx"),
        P("exp", None),
        P("exp", None),
        P("exp", None),
        P("exp", None, None, "ctx"),
        P("exp", "ctx", None),
    )
    out_specs = (P("ctx", "exp"), P("exp", "ctx"))
    return jax.shard_map(
        pair_device if n_ctx == 2 and nz == 4 else on_device,
        mesh=mesh,
        in_specs=in_specs,
        out_specs=out_specs,
        check_vma=False,
    )
```

```python
import jax
import jax.numpy as jnp
from jax import lax
from jax.experimental import pallas as pl
from jax.experimental.pallas import tpu as pltpu
from jax.sharding import PartitionSpec as P

HD = 128
TOP = 6
BF16 = jnp.bfloat16
F32 = jnp.float32


def attend(q_input, k_input, v_input, segment_ids, n_ctx):
    scale = HD ** (-0.5)
    rows = q_input.shape[0]
    heads = q_input.shape[1] // HD
    place = lax.axis_index("ctx") * rows + jnp.arange(rows, dtype=jnp.int32)
    if n_ctx == 2:
        ahead = [(0, 1)]
        keys = jnp.concatenate([lax.ppermute(k_input, "ctx", ahead), k_input], axis=0)
        values = jnp.concatenate([lax.ppermute(v_input, "ctx", ahead), v_input], axis=0)
        docs = jnp.concatenate([lax.ppermute(segment_ids, "ctx", ahead), segment_ids], axis=0)
        first = (lax.axis_index("ctx") - 1) * rows
    else:
        keys = lax.all_gather(k_input, "ctx", axis=0, tiled=True)
        values = lax.all_gather(v_input, "ctx", axis=0, tiled=True)
        docs = lax.all_gather(segment_ids, "ctx", axis=0, tiled=True)
        first = 0
    count = keys.shape[0]
    key_place = first + jnp.arange(count, dtype=jnp.int32)
    visible = (
        (key_place[None, :] <= place[:, None])
        & (key_place[None, :] >= 0)
        & (docs[None, :] == segment_ids[:, None])
    )
    queries = q_input.reshape(rows, heads, HD)
    scores = (
        jnp.einsum(
            "qhd,khd->qhk", queries, keys.reshape(count, heads, HD), preferred_element_type=F32
        )
        * scale
    )
    scores = jnp.where(visible[:, None, :], scores, -1e30)
    newest = jnp.max(scores, axis=2)
    probs = jnp.where(visible[:, None, :], jnp.exp(scores - newest[:, :, None]), 0.0)
    total = jnp.sum(probs, axis=2)
    summed = jnp.einsum(
        "qhk,khd->qhd",
        probs.astype(BF16),
        values.reshape(count, heads, HD),
        preferred_element_type=F32,
    )
    return (summed / total[:, :, None]).reshape(rows, heads * HD).astype(BF16)

SHARED = 2560
OVER_X = 1792
FIRST = [1, 3, 0]
LAST = [2]

VMEM = pl.BlockSpec(memory_space=pltpu.VMEM)
SMEM = pl.BlockSpec(memory_space=pltpu.SMEM)
MIB = 1024 * 1024
LANES = 128
SUBLANES = 16


def call(body, out_shape, flops, moved, room, **kw):
    return pl.pallas_call(
        body,
        out_shape=out_shape,
        compiler_params=pltpu.CompilerParams(vmem_limit_bytes=room * MIB),
        cost_estimate=pl.CostEstimate(flops=flops, bytes_accessed=moved, transcendentals=0),
        **kw,
    )


def prepare(tokens, expert_ids, route_weight, at_x, experts):
    rows, width = tokens.shape
    split = (width - SHARED) // 2

    def body(x_ref, tokens, ids, weights, out, theirs):
        own = pl.ds(pl.multiple_of(SHARED + x_ref[0] * split, LANES), split)
        other = pl.ds(pl.multiple_of(SHARED + (1 - x_ref[0]) * split, LANES), split)
        out[:, :SHARED] = tokens[:, :SHARED]
        out[:, SHARED : SHARED + split] = tokens[:, own]
        theirs[...] = tokens[:, other]
        column = lax.broadcasted_iota(jnp.int32, (LANES, rows), 0)
        expert, term = column % experts, column // experts
        meta = jnp.zeros((LANES, rows), F32)
        for k in range(TOP):
            weight = jnp.broadcast_to(weights[k : k + 1, :], (LANES, rows))
            high = weight.astype(BF16).astype(F32)
            middle = (weight - high).astype(BF16).astype(F32)
            low = weight - high - middle
            value = jnp.where(term == 1, high, jnp.where(term == 2, middle, low))
            value = jnp.where(term == 0, 1.0, value)
            meta = jnp.where((ids[k : k + 1, :] == expert) & (term < 4), value, meta)
        eye = lax.broadcasted_iota(jnp.int32, (LANES, LANES), 0) == lax.broadcasted_iota(
            jnp.int32, (LANES, LANES), 1
        )
        meta = lax.dot_general(
            meta.astype(BF16),
            jnp.where(eye, 1.0, 0.0).astype(BF16),
            (((0,), (0,)), ((), ())),
            preferred_element_type=F32,
        )
        out[:, SHARED + split :] = meta.astype(BF16)

    return call(
        body,
        (
            jax.ShapeDtypeStruct((rows, SHARED + split + LANES), BF16),
            jax.ShapeDtypeStruct((rows, split), BF16),
        ),
        0,
        4 * rows * width,
        8,
        in_specs=[SMEM] + [VMEM] * 3,
        out_specs=(VMEM,) * 2,
    )(at_x.reshape(1), tokens, expert_ids.T, route_weight.T)


def pick(blocks, more, me, at_x, cap):
    count = len(blocks)
    rows, width = blocks[0].shape
    split = more[0].shape[1]
    edge = width - LANES
    features = edge + split
    step = count
    total = count + len(more)

    def body(s_ref, *refs):
        sources, (near, meta, other, placing, wide, *held, done) = refs[:total], refs[total:]
        copies = [
            pltpu.make_async_copy(source, to, done.at[i])
            for i, (source, to) in enumerate(zip(sources, held))
        ]
        for copy in copies:
            copy.start()
        for copy in copies:
            copy.wait()
        ins, extra = held[:count], held[count:]
        mine, x = s_ref[0], s_ref[1]
        lane = lax.broadcasted_iota(jnp.int32, (rows, LANES), 1)
        earlier = lax.broadcasted_iota(jnp.int32, (rows, rows), 0) > lax.broadcasted_iota(
            jnp.int32, (rows, rows), 1
        )
        slot = lax.broadcasted_iota(jnp.int32, (rows, cap), 1).astype(F32)
        own = pl.ds(pl.multiple_of(SHARED + x * split, LANES), split)
        theirs = pl.ds(pl.multiple_of(SHARED + (1 - x) * split, LANES), split)
        pieces = [
            ref[b * rows : (b + 1) * rows, :] for ref in extra for b in range(ref.shape[0] // rows)
        ]
        for begin in range(0, count, step):
            wide[...] = jnp.zeros_like(wide)
            for i in range(begin, begin + step):
                member = ins[i][:, edge:]
                rank = jnp.dot(earlier.astype(BF16), member, preferred_element_type=F32)
                member = member.astype(F32)
                local = i - begin
                for j in range(2):
                    at = lane == (mine if j == 0 else mine + 1 - 2 * (mine % 2))
                    hit = jnp.sum(jnp.where(at, member, 0.0), axis=1, keepdims=True)
                    place = jnp.sum(jnp.where(at, rank, 0.0), axis=1, keepdims=True)
                    onehot = jnp.where((place == slot) & (hit > 0.5), 1.0, 0.0).astype(BF16)
                    placing[i, :, j * cap : (j + 1) * cap] = onehot
                    column = (j * step + local) * cap
                    wide[local * rows : (local + 1) * rows, column : column + cap] = onehot
            onehot = wide[...]
            to = slice(begin * cap, (begin + step) * cap)

            def rows_of(parts):
                got = lax.dot_general(
                    onehot,
                    jnp.concatenate(parts, axis=0),
                    (((0,), (0,)), ((), ())),
                    preferred_element_type=F32,
                ).astype(BF16)
                return got[: step * cap], got[step * cap :]

            these = ins[begin : begin + step]
            near[to, :SHARED], other[to, :SHARED] = rows_of([r[:, :SHARED] for r in these])
            near[to, own], other[to, own] = rows_of([r[:, SHARED:edge] for r in these])
            near[to, theirs], other[to, theirs] = rows_of(pieces[begin : begin + step])
            meta[to, :], other[to, features:] = rows_of([r[:, edge:] for r in these])

    shape = lambda *s: jax.ShapeDtypeStruct(s, BF16)
    return call(
        body,
        (
            shape(count * cap, features),
            shape(count * cap, LANES),
            shape(count * cap, features + LANES),
            shape(count, rows, 2 * cap),
        ),
        40 * count * cap * rows * features,
        2 * count * (rows + 2 * cap) * features,
        20,
        in_specs=[SMEM] + [pl.BlockSpec(memory_space=pltpu.HBM)] * total,
        out_specs=(VMEM,) * 4,
        scratch_shapes=[pltpu.VMEM((step * rows, 2 * step * cap), BF16)]
        + [pltpu.VMEM(a.shape, BF16) for a in (*blocks, *more)]
        + [pltpu.SemaphoreType.DMA((total,))],
    )(jnp.stack([me, at_x]), *blocks, *more)


def mix(placing, near, far, far_first, first, count, at_x, late, adds=(), dtype=BF16):
    _, rows, both = placing.shape
    cap = both // 2
    half = near.shape[1] // 2
    rest = half - OVER_X
    width = OVER_X if late else half + rest

    def body(x_ref, placing, near, far, *refs):
        out = refs[-1]
        own = pl.multiple_of(x_ref[0] * half, LANES)
        other = pl.multiple_of((1 - x_ref[0]) * half, LANES)
        if late:
            parts = [(other, OVER_X, 0)]
        else:
            parts = [
                (own, OVER_X, 0),
                (pl.multiple_of(own + OVER_X, LANES), rest, OVER_X),
                (pl.multiple_of(other + OVER_X, LANES), rest, half),
            ]
        for start, size, to in parts:
            columns = pl.ds(start, size)
            slots = jnp.concatenate([near[:, columns], far[:, columns]], axis=0)
            total = jnp.dot(placing[0], slots, preferred_element_type=F32)
            for ref in refs[:-1]:
                if to + size <= ref.shape[1]:
                    total = total + ref[:, to : to + size].astype(F32)
            out[:, to : to + size] = total.astype(dtype)

    def at(base):
        return lambda g: (g + base, 0)

    return call(
        body,
        jax.ShapeDtypeStruct((count * rows, width), dtype),
        4 * count * rows * cap * width,
        2 * count * (rows + 2 * cap) * width,
        12,
        grid=(count,),
        in_specs=[
            SMEM,
            pl.BlockSpec((1, rows, both), lambda g: (g + first, 0, 0)),
            pl.BlockSpec((cap, 2 * half), at(first)),
            pl.BlockSpec((cap, 2 * half), at(first - far_first)),
        ]
        + [pl.BlockSpec((rows, a.shape[1]), at(base)) for a, base in adds],
        out_specs=pl.BlockSpec((rows, width), at(0)),
    )(at_x.reshape(1), placing, near, far, *[a for a, _ in adds])


def attend_pair(q_input, k_input, v_input, segment_ids, past, at_x):
    rows, width = q_input.shape
    scale = HD ** (-0.5)
    turn = (((1,), (1,)), ((), ()))

    def body(x_ref, q, k, v, down, along, past_k, past_v, past_docs, out, bias):
        @pl.when(pl.program_id(0) == 0)
        def _():
            i = lax.broadcasted_iota(jnp.int32, (rows, rows), 0)
            j = lax.broadcasted_iota(jnp.int32, (rows, rows), 1)
            same = down[...] == past_docs[:1, :].astype(F32)
            bias[:, :rows] = jnp.where(same & (x_ref[0] > 0), 0.0, -1e30)
            bias[:, rows:] = jnp.where((down[...] == along[...]) & (j <= i), 0.0, -1e30)

        query = q[...]
        early = lax.dot_general(query, past_k[...], turn, preferred_element_type=F32)
        late = lax.dot_general(query, k[...], turn, preferred_element_type=F32)
        early = early * scale + bias[:, :rows]
        late = late * scale + bias[:, rows:]
        top = jnp.maximum(
            jnp.max(early, axis=1, keepdims=True), jnp.max(late, axis=1, keepdims=True)
        )
        early, late = jnp.exp(early - top), jnp.exp(late - top)
        total = jnp.sum(early, axis=1, keepdims=True) + jnp.sum(late, axis=1, keepdims=True)
        mixed = jnp.dot(early.astype(BF16), past_v[...], preferred_element_type=F32) + jnp.dot(
            late.astype(BF16), v[...], preferred_element_type=F32
        )
        out[...] = (mixed / total).astype(BF16)

    heads = width // HD
    head = pl.BlockSpec((rows, HD), lambda h: (0, h))
    return call(
        body,
        jax.ShapeDtypeStruct((rows, width), BF16),
        48 * rows * rows * width,
        14 * rows * width,
        14,
        grid=(heads,),
        in_specs=[
            SMEM,
            head,
            head,
            head,
            pl.BlockSpec((rows, 1), lambda h: (0, 0)),
            pl.BlockSpec((1, rows), lambda h: (0, 0)),
            head,
            pl.BlockSpec((rows, HD), lambda h: (1, h)),
            pl.BlockSpec((SUBLANES, rows), lambda h: (2 * rows // SUBLANES, 0)),
        ],
        out_specs=head,
        scratch_shapes=[pltpu.VMEM((rows, 2 * rows), F32)],
    )(
        at_x.reshape(1),
        q_input,
        k_input,
        v_input,
        segment_ids.astype(F32)[:, None],
        segment_ids.astype(F32)[None, :],
        past,
        past,
        past,
    )


def spread(onehot):
    blocks, cap, rows = onehot.shape
    same = jnp.eye(blocks, dtype=jnp.bool_)
    wide = onehot[:, :, None, :] & same[:, None, :, None]
    return wide.reshape(blocks * cap, blocks * rows).astype(BF16)


def solution(mesh):
    n_ctx = mesh.shape["ctx"]
    n_exp = mesh.shape["exp"]
    nz = n_exp // 4

    def pairs(move):
        out = []
        for i in range(n_exp):
            z, y, c = i // 4, (i // 2) % 2, i % 2
            z, y, c = move(z, y, c)
            out.append((i, (z % nz * 2 + y) * 2 + c))
        return out

    def z_shift(x, d):
        return lax.ppermute(x, "exp", pairs(lambda z, y, c: (z + d, y, c)))

    def y_swap(x):
        return lax.ppermute(x, "exp", pairs(lambda z, y, c: (z, 1 - y, c)))

    def core_swap(x):
        return lax.ppermute(x, "exp", pairs(lambda z, y, c: (z, y, 1 - c)))

    def x_swap(x):
        return lax.ppermute(x, "ctx", [(0, 1), (1, 0)])

    def on_device(
        q_input, k_input, v_input, segment_ids, tokens, expert_ids, route_weight, w_in, w_down
    ):
        me = lax.axis_index("exp")
        at_x = lax.axis_index("ctx")
        rows, width = tokens.shape
        cap = rows * 8 // n_exp
        half = width // 2
        near = n_exp // 2
        slots = near * cap

        if n_ctx == 2:
            plan = [("x", 1024), ("x", 1024), ("", 1024), ("x", 1024), ("", 1024)]
        else:
            plan = [("", width)]
        arrived = []
        start = 0
        for kind, size in plan:
            if kind == "x":
                block = lax.dynamic_slice_in_dim(tokens, start + at_x * (size // 2), size // 2, 1)
            else:
                block = tokens[:, start : start + size]
            line = jnp.concatenate([block] + [z_shift(block, d) for d in range(1, nz)], axis=0)
            both = jnp.concatenate([line, y_swap(line)], axis=0)
            if kind == "x":
                other = x_swap(both)
                both = jnp.concatenate(
                    [jnp.where(at_x == 0, both, other), jnp.where(at_x == 0, other, both)], axis=1
                )
            arrived.append((start, size, both))
            start += size

        meta = jnp.concatenate([expert_ids.astype(F32), route_weight], axis=1)
        meta = lax.all_gather(meta, "exp", axis=0, tiled=False)
        z, y, c = me // 4, (me // 2) % 2, me % 2
        order = jnp.stack(
            [
                ((z - d + nz) % nz * 2 + (y + yr) % 2) * 2 + (c + cr) % 2
                for cr in range(2)
                for yr in range(2)
                for d in range(nz)
            ]
        )
        meta = meta[order]
        ids, weights = meta[:, :, :TOP].astype(jnp.int32), meta[:, :, TOP:]

        def placing(ids, expert):
            named = ids == expert
            hit = jnp.any(named, axis=2)
            count = hit.astype(jnp.int32)
            rank = jnp.cumsum(count, axis=1) - count
            slot = jnp.arange(cap, dtype=jnp.int32)
            return named, hit[:, None, :] & (rank[:, None, :] == slot[None, :, None])

        named, mine = placing(ids, me)
        _, others = placing(ids[:near], me + 1 - 2 * c)
        weight = jnp.sum(jnp.where(named, weights, 0.0), axis=2)
        weight = jnp.sum(jnp.where(mine, weight[:, None, :], 0.0), axis=2).reshape(2 * slots, 1)
        place = jnp.concatenate([spread(mine[:near]), spread(others)], axis=0)

        gate = up = None
        for start, size, both in arrived:
            placed = jnp.dot(place, both, preferred_element_type=F32).astype(BF16)
            block = jnp.concatenate([placed[:slots], core_swap(placed[slots:])], axis=0)
            g = jnp.dot(block, w_in[0, 0, start : start + size], preferred_element_type=F32)
            u = jnp.dot(block, w_in[0, 1, start : start + size], preferred_element_type=F32)
            gate = g if gate is None else gate + g
            up = u if up is None else up + u
        hidden = (jax.nn.silu(gate) * up).astype(BF16)

        if n_ctx == 2:
            back = [("x", 512), ("x", 512), ("", 512), ("x", 512), ("", 512)]
        else:
            back = [("", half)]
        down = w_down[0]
        pieces = []
        start = 0
        for kind, size in back:
            if n_ctx == 2:
                cols = jnp.concatenate(
                    [down[:, start : start + size], down[:, half + start : half + start + size]],
                    axis=1,
                )
            else:
                cols = down
            part = jnp.dot(hidden, cols, preferred_element_type=F32)
            part = (part * weight).astype(BF16)
            part = jnp.concatenate([part[:slots], core_swap(part[slots:])], axis=0)
            summed = lax.dot_general(
                place, part, (((0,), (0,)), ((), ())), preferred_element_type=F32
            )

            def over_x(summed):
                first, second = summed[:, :size].astype(BF16), summed[:, size:].astype(BF16)
                other = x_swap(jnp.where(at_x == 0, second, first))
                own = jnp.where(at_x == 0, summed[:, :size], summed[:, size:])
                return own + other.astype(F32)

            if kind == "x":
                summed = over_x(summed)
            count = nz * rows
            summed = summed[:count] + y_swap(summed[count:].astype(BF16)).astype(F32)
            total = summed[:rows]
            for d in range(1, nz):
                block = summed[d * rows : (d + 1) * rows].astype(BF16)
                total = total + z_shift(block, -d).astype(F32)
            if kind != "x":
                if n_ctx == 2:
                    total = over_x(total)
                else:
                    total = lax.psum_scatter(
                        total.astype(BF16), "ctx", scatter_dimension=1, tiled=True
                    )
            pieces.append(total.astype(BF16))
            start += size
        moe_out = jnp.concatenate(pieces, axis=1)
        attn_out = attend(q_input, k_input, v_input, segment_ids, n_ctx)
        return attn_out, moe_out

    def pair_device(
        q_input, k_input, v_input, segment_ids, tokens, expert_ids, route_weight, w_in, w_down
    ):
        if q_input.shape[0] != q_input.shape[1]:
            return on_device(
                q_input,
                k_input,
                v_input,
                segment_ids,
                tokens,
                expert_ids,
                route_weight,
                w_in,
                w_down,
            )
        me = lax.axis_index("exp")
        at_x = lax.axis_index("ctx")
        rows, width = tokens.shape
        cap = rows * 8 // n_exp
        half = width // 2
        split = (width - SHARED) // 2
        after = lax.optimization_barrier

        block, theirs = prepare(tokens, expert_ids, route_weight, at_x, n_exp)
        cut = lambda a: a[:, SHARED : SHARED + split]
        both = lambda d: jnp.concatenate([cut(line[d]), cut(across[d])], axis=0)
        line = {0: block, 1: z_shift(block, 1)}
        across = {0: y_swap(block)}
        line[1], again = after((line[1], block))
        line[3] = z_shift(again, -1)
        line[3], again = after((line[3], line[1]))
        line[2] = z_shift(again, 1)
        block, k_input = after((block, k_input))
        docs = jnp.broadcast_to(segment_ids.astype(BF16)[None, :], (SUBLANES, k_input.shape[1]))
        past = lax.ppermute(jnp.concatenate([k_input, v_input, docs], axis=0), "ctx", [(0, 1)])
        line[1], across[0] = after((line[1], across[0]))
        across[1] = y_swap(line[1])
        line[3], across[1] = after((line[3], across[1]))
        across[3] = y_swap(line[3])
        across[0], past = after((across[0], past))
        more = {0: [theirs, x_swap(cut(across[0]))], 1: [x_swap(both(1))]}
        line[2], across[3], before = after((line[2], across[3], more[0][1]))
        more[0][1] = before
        across[2] = y_swap(line[2])
        more[3] = [x_swap(both(3))]
        line[2], before = after((line[2], more[1][0]))
        more[1] = [before]
        attn_out = attend_pair(q_input, k_input, v_input, segment_ids, past, at_x)
        across[2], before, attn_out = after((across[2], more[3][0], attn_out))
        more[3] = [before]
        more[2] = [x_swap(both(2))]

        def place(group, extra):
            return pick(
                [b for d in group for b in (line[d], across[d])], extra, me, at_x, cap
            )

        early, early_meta, early_sent, early_placing = place(
            FIRST, [a for d in FIRST for a in more[d]]
        )
        early_far = core_swap(early_sent)
        more[2][0], early = after((more[2][0], early))
        near, meta, sent, placing = place(LAST, more[2])
        far = core_swap(sent)
        join = lambda *parts: jnp.concatenate(parts, axis=0)
        placing = join(placing, early_placing)
        near, meta = join(near, early), join(meta, early_meta)
        far = join(far, early_far)

        def expert(block, meta):
            gate = jnp.dot(block, w_in[0, 0], preferred_element_type=F32)
            up = jnp.dot(block, w_in[0, 1], preferred_element_type=F32)
            gate, up = after((gate, up))
            hidden = (jax.nn.silu(gate) * up).astype(BF16)
            lane = jnp.arange(LANES, dtype=jnp.int32)
            at = (lane % n_exp == me) & (lane >= n_exp) & (lane < 4 * n_exp)
            scale = jnp.sum(jnp.where(at, meta.astype(F32), 0.0), axis=1, keepdims=True)
            hidden, scale = after((hidden, scale))
            out = jnp.dot(hidden, w_down[0], preferred_element_type=F32)
            return (out * scale).astype(BF16)

        near = expert(near, meta)
        near, far = after((near, far))
        sent = expert(far[:, :width], far[:, width:])
        edge = sent.shape[0] // 2
        far_a = core_swap(sent[:edge])
        far_a, rest = after((far_a, sent[edge:]))
        far_b = core_swap(rest)

        def sums(i, count, late, adds=(), dtype=BF16):
            far, begin = (far_a, 0) if i < 4 else (far_b, 4)
            return mix(placing, near, far, begin, i, count, at_x, late, adds, dtype)

        got_x = []
        for i in range(4):
            late = sums(2 * i, 2, True)
            near, late = after((near, late))
            got_x.append(x_swap(late))

        def over_y(i):
            return y_swap(sums(2 * i + 1, 1, False, [(got_x[i], 1)]))

        got_y = [over_y(0)]
        turn = sums(3, 1, False, [(got_x[1], 1)])
        got_y[0], turn = after((got_y[0], turn))
        got_y.append(y_swap(turn))
        part = sums(0, 1, False, [(got_x[0], 0), (got_y[0], 0)])
        part = z_shift(part, -1)
        got_x[2], part = after((got_x[2], part))
        got_y.append(over_y(2))
        part = sums(2, 1, False, [(got_x[1], 0), (got_y[1], 0), (part, 0)])
        right = z_shift(part, -1)
        got_x[3], right = after((got_x[3], right))
        got_y.append(over_y(3))
        left = z_shift(sums(4, 1, False, [(got_x[2], 0), (got_y[2], 0)]), 1)
        total = sums(6, 1, False, [(got_x[3], 0), (got_y[3], 0)], F32)
        total = total + right.astype(F32) + left.astype(F32)
        got = x_swap(total[:, half:].astype(BF16))
        moe_out = jnp.concatenate(
            [total[:, :OVER_X], total[:, OVER_X:half] + got.astype(F32)], axis=1
        ).astype(BF16)
        return attn_out, moe_out

    in_specs = (
        P("ctx", "exp"),
        P("ctx", "exp"),
        P("ctx", "exp"),
        P("ctx"),
        P("exp", None),
        P("exp", None),
        P("exp", None),
        P("exp", None, None, "ctx"),
        P("exp", "ctx", None),
    )
    out_specs = (P("ctx", "exp"), P("exp", "ctx"))
    return jax.shard_map(
        pair_device if n_ctx == 2 and nz == 4 else on_device,
        mesh=mesh,
        in_specs=in_specs,
        out_specs=out_specs,
        check_vma=False,
    )
```
